256 devices in a mesh: section: 4 (over y), expert: 64 (over z, x, core).
Axes of the slice: x: 4, y: 4, z: 8, core: 2. Of those that a mesh axis runs over, the one named last changes fastest.
Arguments:
- hidden: bfloat16 [4, 4096, 4096], P('section', 'expert'), may hold values from -6 to 6
- queries: bfloat16 [4, 4096, 4096], P('section', 'expert'), may hold values from -10 to 10
- fresh_kv: bfloat16 [4, 2, 4096, 256], P('section', None, 'expert'), may hold values from -10 to 10
- cache_kv: bfloat16 [4, 2, 2048, 256], P('section', None, 'expert'), may hold values from -10 to 10
- cache_fill: int32 [4], P('section'), may hold values from 1024 to 2048, as said below
- out_proj: bfloat16 [4, 4096, 4096], P('section', 'expert'), may hold values from -0.375 to 0.375
- norm_gain: bfloat16 [4, 4096], P('section'), may hold values from 0.5 to 1.5
- router_weight: bfloat16 [4, 4096, 128], P('section'), may hold values from -3 to 3
- expert_labels: int32 [4, 4096, 8], P('section', 'expert'), may hold values from 0 to 127, as said below
- gate_proj: bfloat16 [4, 64, 4096, 384], P('section', 'expert'), may hold values from -0.09375 to 0.09375
- up_proj: bfloat16 [4, 64, 4096, 384], P('section', 'expert'), may hold values from -0.09375 to 0.09375
- down_proj: bfloat16 [4, 64, 384, 4096], P('section', 'expert'), may hold values from -0.15625 to 0.15625
Outputs:
- passed: bfloat16 [4, 4096, 4096], P('section', 'expert')
The draws below stay inside these ranges and needn't reach their ends.
Inputs may be any that keep to these rules, and one draw needn't show every extreme that they name: `expert_labels`: each row names 8 different experts, exactly one of them below 16. At most 8 of the 64 tokens of one device name one expert below 16, and on every device some expert is named by 8 of them. `cache_fill`: at least 1024; some section has 2048.
All inputs are finite; a program needn't handle non-finite values.
Results may differ from the reference program's by a relative error of at most 0.008.
Values may be sent and summed in bfloat16 or wider, within the bound.
No kernel may reach another device: no remote copies, remote signals or barrier semaphores. Data moves between devices by JAX's collectives and lax.ppermute only.
A program may use at most 256 MiB of HBM per device.

```python
import math
import jax
import jax.numpy as jnp
from jax import lax

D = 4096
QUERY_HEADS = 32
KEY_VALUE_HEADS = 2
HEAD_SIZE = 128
EXPERTS = 128
TOPK = 8
FF = 1536
SPLIT = 4
TOK_DEV = 64
RELAY_SECTIONS = 4
EXPERTS_AIRBORNE = 16
FF_DEV = 384
CAP = 8
TOKENS = 4096
CACHE = 2048
N_EXPERT = 64


def draw_queries(key, part):
    key = jax.random.fold_in(key, 3)
    array_shape = (RELAY_SECTIONS, TOKENS, QUERY_HEADS * HEAD_SIZE)
    values = jnp.clip(jax.random.normal(key, array_shape, jnp.float32), -10.0, 10.0)
    return values.astype(jnp.bfloat16)


def key_value_pair(key, row_block):
    key_part, value_part = jax.random.split(key)
    array_shape = (RELAY_SECTIONS, 1, row_block, KEY_VALUE_HEADS * HEAD_SIZE)
    values = jnp.clip(jax.random.normal(value_part, array_shape, jnp.float32), -10.0, 10.0)
    keys_drawn = jnp.clip(jax.random.normal(key_part, array_shape, jnp.float32), -10.0, 10.0)
    return jnp.concatenate([keys_drawn, values], axis=1).astype(jnp.bfloat16)


def draw_fresh_kv(key, part):
    key = jax.random.fold_in(key, 5)
    return key_value_pair(key, TOKENS)


def draw_cache_kv(key, part):
    key = jax.random.fold_in(key, 7)
    return key_value_pair(key, CACHE)


def draw_cache_fill(key, part):
    key = jax.random.fold_in(key, 9)
    first, second = jax.random.split(key)
    fills = jax.random.randint(first, (RELAY_SECTIONS,), CACHE // 2, CACHE + 1)
    full_section = jax.random.randint(second, (), 0, RELAY_SECTIONS)
    return jnp.where(jnp.arange(RELAY_SECTIONS) == full_section, CACHE, fills).astype(jnp.int32)


def draw_router_weight(key, part):
    key = jax.random.fold_in(key, 13)
    array_shape = (RELAY_SECTIONS, D, EXPERTS)
    values = jnp.clip(jax.random.normal(key, array_shape, jnp.float32) / D ** 0.5, -3.0, 3.0)
    return values.astype(jnp.bfloat16)


def block_picks(key, hot_expert):
    order_key, others_key = jax.random.split(key)
    rank = jax.random.permutation(order_key, TOK_DEV)
    others = jax.random.permutation(others_key, EXPERTS_AIRBORNE - 1)
    other_pick = others[jnp.maximum(rank - CAP, 0) % (EXPERTS_AIRBORNE - 1)]
    other_pick = other_pick + (other_pick >= hot_expert).astype(jnp.int32)
    return jnp.where(rank < CAP, hot_expert, other_pick).astype(jnp.int32)


def token_vector(key, airborne_label):
    perm_key, roll_key = jax.random.split(key)
    outside_mask = jax.random.permutation(perm_key, EXPERTS - EXPERTS_AIRBORNE)[:TOPK - 1] + EXPERTS_AIRBORNE
    current_row = jnp.concatenate([airborne_label[None], outside_mask.astype(jnp.int32)])
    return jnp.roll(current_row, jax.random.randint(roll_key, (), 0, TOPK))


def draw_expert_labels(key, part):
    key = jax.random.fold_in(key, 11)
    hot_key, block_key, row_key = jax.random.split(key, 3)
    hot_experts = jax.random.randint(hot_key, (RELAY_SECTIONS,), 0, EXPERTS_AIRBORNE)
    cache_blocks = TOKENS // TOK_DEV
    block_keys = jax.random.split(block_key, RELAY_SECTIONS * cache_blocks)
    hot_each = jnp.repeat(hot_experts, cache_blocks)
    picks = jax.vmap(block_picks)(block_keys, hot_each).reshape(RELAY_SECTIONS * TOKENS)
    row_keys = jax.random.split(row_key, RELAY_SECTIONS * TOKENS)
    row_block = jax.vmap(token_vector)(row_keys, picks)
    return row_block.reshape(RELAY_SECTIONS, TOKENS, TOPK).astype(jnp.int32)


def block_levels(rng, dims, pieces, low, largest):
    def one(axis_at, parts):
        steps = jax.random.uniform(jax.random.fold_in(jax.random.fold_in(rng, 6), axis_at), (parts,), jnp.float32, low / len(pieces), largest / len(pieces))
        return jnp.repeat(jnp.exp(steps), dims[axis_at] // parts).reshape((-1,) + (1,) * (len(dims) - axis_at - 1))

    gain = one(*pieces[0])
    for cut in pieces[1:]:
        gain = gain * one(*cut)
    return gain


def centred(stream_key, shape, deviation, reach, cuts=(), kind=jnp.bfloat16):
    result = deviation * jax.random.normal(stream_key, shape, jnp.float32)
    if cuts:
        result = result * block_levels(stream_key, shape, cuts, -0.22, 0.18)
    return jnp.clip(result, -reach, reach).astype(kind)


def setup_inputs(seed: int = 0) -> dict:
    seeds = jax.random.split(jax.random.key(seed), 13)
    return {
        "hidden": centred(seeds[0], (RELAY_SECTIONS, TOKENS, D), 1.0, 6.0, ((0, 4), (1, 64))),
        "queries": draw_queries(jax.random.fold_in(seeds[12], 71), 0),
        "fresh_kv": draw_fresh_kv(jax.random.fold_in(seeds[12], 71), 0),
        "cache_kv": draw_cache_kv(jax.random.fold_in(seeds[12], 71), 0),
        "cache_fill": draw_cache_fill(jax.random.fold_in(seeds[12], 71), 0),
        "out_proj": centred(seeds[5], (RELAY_SECTIONS, QUERY_HEADS * HEAD_SIZE, D), (QUERY_HEADS * HEAD_SIZE // 16) ** -0.5, 0.375, ((0, 4), (1, 64))),
        "norm_gain": jnp.clip(1.0 + 0.1 * jax.random.normal(seeds[6], (RELAY_SECTIONS, D), jnp.float32), 0.5, 1.5).astype(jnp.bfloat16),
        "router_weight": draw_router_weight(jax.random.fold_in(seeds[12], 71), 0),
        "expert_labels": draw_expert_labels(jax.random.fold_in(seeds[12], 71), 0),
        "gate_proj": centred(seeds[9], (RELAY_SECTIONS, N_EXPERT, D, FF_DEV), D ** -0.5, 0.09375, ((0, 4), (1, 64))),
        "up_proj": centred(seeds[10], (RELAY_SECTIONS, N_EXPERT, D, FF_DEV), D ** -0.5, 0.09375, ((0, 4), (1, 64))),
        "down_proj": centred(seeds[11], (RELAY_SECTIONS, N_EXPERT, FF_DEV, D), FF ** -0.5, 0.15625, ((0, 4), (1, 64))),
    }


def attend_section(queries, fresh_kv, cache_kv, fill):
    cache_length = CACHE + TOKENS
    joined_rows = jnp.concatenate([cache_kv, fresh_kv], axis=1)
    gathered_keys = joined_rows[0].reshape(cache_length, KEY_VALUE_HEADS, HEAD_SIZE)
    gathered_values = joined_rows[1].reshape(cache_length, KEY_VALUE_HEADS, HEAD_SIZE)
    gathered_queries = queries.reshape(TOKENS, QUERY_HEADS, HEAD_SIZE)
    column = jnp.arange(cache_length, dtype=jnp.int32)[None, :]
    row_pos = jnp.arange(TOKENS, dtype=jnp.int32)[:, None]
    visible = jnp.where(column < CACHE, column < fill, column - CACHE <= row_pos)
    head_group = QUERY_HEADS // KEY_VALUE_HEADS
    scale = 1.0 / math.sqrt(HEAD_SIZE)

    def one_head(head):
        kv_head = head // head_group
        query_head = lax.dynamic_index_in_dim(gathered_queries, head, 1, keepdims=False)
        key_head = lax.dynamic_index_in_dim(gathered_keys, kv_head, 1, keepdims=False)
        value_head = lax.dynamic_index_in_dim(gathered_values, kv_head, 1, keepdims=False)
        scores = jnp.dot(query_head, key_head.T, preferred_element_type=jnp.float32) * scale
        masked = jnp.where(visible, scores, -1e+30)
        highest = lax.optimization_barrier(jnp.max(masked, axis=1, keepdims=True))
        weights = jnp.where(visible, jnp.exp(masked - highest), 0.0)
        totals = lax.optimization_barrier(jnp.sum(weights, axis=1, keepdims=True))
        rounded = weights.astype(jnp.bfloat16)
        return jnp.dot(rounded, value_head, preferred_element_type=jnp.float32) / totals
    heads_out = lax.map(one_head, jnp.arange(QUERY_HEADS, dtype=jnp.int32))
    return jnp.transpose(heads_out, (1, 0, 2)).reshape(TOKENS, QUERY_HEADS * HEAD_SIZE).astype(jnp.bfloat16)

def section_layer(hidden, queries, fresh_kv, cache_kv, fill, out_proj, norm_gain, router_weight, expert_labels, gate_proj, up_proj, down_proj):
    attended = attend_section(queries, fresh_kv, cache_kv, fill)
    projected = jnp.dot(attended, out_proj, preferred_element_type=jnp.float32)
    mixed = hidden.astype(jnp.float32) + projected
    inverse = lax.rsqrt(lax.optimization_barrier(jnp.mean(mixed * mixed, axis=1, keepdims=True)) + 1e-06)
    normed = (mixed * inverse * norm_gain.astype(jnp.float32)[None, :]).astype(jnp.bfloat16)
    logits = jnp.dot(normed, router_weight, preferred_element_type=jnp.float32)
    picked = jnp.take_along_axis(logits, expert_labels, axis=1)
    probabilities = jax.nn.softmax(picked, axis=1)
    airborne_mask = expert_labels < EXPERTS_AIRBORNE
    selected_experts = lax.optimization_barrier(jnp.sum(jnp.where(airborne_mask, expert_labels, 0), axis=1)).astype(jnp.int32)
    merge_results = lax.optimization_barrier(jnp.sum(jnp.where(airborne_mask, probabilities, 0.0), axis=1))
    gate_full = jnp.transpose(gate_proj.reshape(EXPERTS_AIRBORNE, SPLIT, D, FF_DEV), (0, 2, 1, 3)).reshape(EXPERTS_AIRBORNE, D, FF)
    up_full = jnp.transpose(up_proj.reshape(EXPERTS_AIRBORNE, SPLIT, D, FF_DEV), (0, 2, 1, 3)).reshape(EXPERTS_AIRBORNE, D, FF)
    down_full = down_proj.reshape(EXPERTS_AIRBORNE, FF, D)
    most_rows = N_EXPERT * CAP

    def one_expert(expert):
        hits = selected_experts == expert
        members = jnp.nonzero(hits, size=most_rows, fill_value=0)[0].astype(jnp.int32)
        valid = jnp.arange(most_rows, dtype=jnp.int32) < jnp.sum(hits.astype(jnp.int32))
        row_block = normed[members]
        gate_mat = lax.dynamic_index_in_dim(gate_full, expert, 0, keepdims=False)
        up_mat = lax.dynamic_index_in_dim(up_full, expert, 0, keepdims=False)
        down_mat = lax.dynamic_index_in_dim(down_full, expert, 0, keepdims=False)
        gated = jnp.dot(row_block, gate_mat, preferred_element_type=jnp.float32)
        lifted = jnp.dot(row_block, up_mat, preferred_element_type=jnp.float32)
        activation = (jax.nn.silu(gated) * lifted).astype(jnp.bfloat16)
        output = jnp.dot(activation, down_mat, preferred_element_type=jnp.float32)
        return (jnp.where(valid[:, None], output, 0.0), members)
    outputs, members = lax.map(one_expert, jnp.arange(EXPERTS_AIRBORNE, dtype=jnp.int32))
    routed = jnp.zeros((TOKENS, D), jnp.float32).at[members.reshape(-1)].add(outputs.reshape(-1, D))
    return (mixed + merge_results[:, None] * routed).astype(jnp.bfloat16)

def reference(hidden, queries, fresh_kv, cache_kv, cache_fill, out_proj, norm_gain, router_weight, expert_labels, gate_proj, up_proj, down_proj):
    results = []
    for section in range(RELAY_SECTIONS):
        results.append(section_layer(hidden[section], queries[section], fresh_kv[section], cache_kv[section], cache_fill[section], out_proj[section], norm_gain[section], router_weight[section], expert_labels[section], gate_proj[section], up_proj[section], down_proj[section]))
    return jnp.stack([results[(section - 1) % RELAY_SECTIONS] for section in range(RELAY_SECTIONS)], axis=0)
```

```python
import functools
import math

import jax
import jax.numpy as jnp
from jax import lax
from jax.experimental import pallas as pl
from jax.experimental.pallas import tpu as pltpu
from jax.sharding import Mesh
from jax.sharding import PartitionSpec as P

EXPERTS = 128
HEAD_SIZE = 128
SPLIT = 4
CHIPS_X = 4
X = ("xh", "xl")
EXPERT = ("z", "xh", "xl", "core")
GROUP = ("z", "xh")


def shifted(shard, axis, by):
    length = lax.axis_size(axis)
    return lax.ppermute(shard, axis, [(i, (i + by) % length) for i in range(length)])


def swapped(shard, axis):
    return lax.ppermute(shard, axis, [(0, 1), (1, 0)])


def in_order(index, own, other, axis):
    return jnp.where(
        index == 0,
        jnp.concatenate([own, other], axis=axis),
        jnp.concatenate([other, own], axis=axis),
    )


def pick(array, index, axis=0):
    return lax.dynamic_index_in_dim(array, index, axis, keepdims=False)


def attention_kernel(planes, columns, block, info_ref, query_ref, *refs):
    key_blocks = refs[:planes]
    value_blocks = refs[planes : planes + columns]
    out_ref, keys, values, top, total, acc = refs[planes + columns :]
    z, x, fill, first = info_ref[0], info_ref[1], info_ref[2], info_ref[3]
    local = key_blocks[0].shape[2]
    fresh = (2 * local) // 3
    cached = local - fresh
    cache_rows = 2 * planes * columns * cached
    pairs = query_ref.shape[0] // 2
    half = HEAD_SIZE // 2
    for k in range(planes):
        plane = lax.rem(z - k + planes, planes)
        for r in range(columns):
            chip = plane * columns + lax.rem(x - r + columns, columns)
            at_cache = pl.multiple_of(chip * 2 * cached, 2 * cached)
            at_fresh = pl.multiple_of(cache_rows + chip * 2 * fresh, 2 * fresh)
            for held, part in ((keys, key_blocks[k].at[r]), (values, value_blocks[r].at[k])):
                held[pl.ds(at_cache, 2 * cached), :] = part[:, :cached, :].reshape(
                    2 * cached, HEAD_SIZE
                )
                held[pl.ds(at_fresh, 2 * fresh), :] = part[:, cached:, :].reshape(
                    2 * fresh, HEAD_SIZE
                )
    rate = math.log2(math.e) / math.sqrt(HEAD_SIZE)

    def visit(pair, start, visible):
        for u in range(2):
            scores = lax.dot_general(
                query_ref[2 * pair + u],
                keys[pl.ds(start, block), :],
                (((1,), (1,)), ((), ())),
                preferred_element_type=jnp.float32,
            )
            if visible is not None:
                mask = visible(scores.shape)
                scores = jnp.where(mask, scores, -1e30)
            before = top[u]
            high = jnp.maximum(before, jnp.max(scores, axis=1, keepdims=True))
            weights = jnp.exp2((scores - high) * rate)
            if visible is not None:
                weights = jnp.where(mask, weights, 0.0)
            factor = jnp.exp2((before - high) * rate)
            part = weights[:, :128]
            for n in range(1, block // 128):
                part = part + weights[:, n * 128 : (n + 1) * 128]
            total[u] = total[u] * factor + part
            top[u] = high
            acc[u] = acc[u] * factor + jnp.dot(
                weights.astype(jnp.bfloat16),
                values[pl.ds(start, block), :],
                preferred_element_type=jnp.float32,
            )

    def one_pair(pair, unused):
        top[...] = jnp.full_like(top, -1e30)
        total[...] = jnp.zeros_like(total)
        acc[...] = jnp.zeros_like(acc)

        def plain(base):
            def body(n, unused):
                visit(pair, pl.multiple_of(base + n * block, block), None)
                return unused

            return body

        full = fill // block
        lax.fori_loop(0, full, plain(0), 0)

        @pl.when(fill > full * block)
        def _():
            start = pl.multiple_of(full * block, block)
            visit(
                pair,
                start,
                lambda shape: start + lax.broadcasted_iota(jnp.int32, shape, 1) < fill,
            )

        done = first // block
        lax.fori_loop(0, done, plain(cache_rows), 0)
        ahead = done * block - first
        visit(
            pair,
            pl.multiple_of(cache_rows + done * block, block),
            lambda shape: ahead + lax.broadcasted_iota(jnp.int32, shape, 1)
            <= lax.broadcasted_iota(jnp.int32, shape, 0),
        )
        heads = [
            (acc[u] / jnp.sum(total[u], axis=1, keepdims=True)).astype(out_ref.dtype)
            for u in range(2)
        ]
        at = pl.multiple_of(pair * 2 * half, 2 * half)
        for n in range(2):
            out_ref[n, :, pl.ds(at, 2 * half)] = jnp.concatenate(
                [head[:, n * half : (n + 1) * half] for head in heads], axis=1
            )
        return unused

    lax.fori_loop(0, pairs, one_pair, 0)


def attend(info, queries, key_blocks, value_blocks, block):
    planes, columns = len(key_blocks), len(value_blocks)
    heads, rows, unused = queries.shape
    total_rows = planes * columns * 2 * key_blocks[0].shape[2]
    return pl.pallas_call(
        functools.partial(attention_kernel, planes, columns, block),
        out_shape=jax.ShapeDtypeStruct((2, rows, heads * HEAD_SIZE // 2), jnp.bfloat16),
        in_specs=[pl.BlockSpec(memory_space=pltpu.SMEM)]
        + [pl.BlockSpec(memory_space=pltpu.VMEM)] * (1 + planes + columns),
        out_specs=pl.BlockSpec(memory_space=pltpu.VMEM),
        scratch_shapes=[
            pltpu.VMEM((total_rows, HEAD_SIZE), jnp.bfloat16),
            pltpu.VMEM((total_rows, HEAD_SIZE), jnp.bfloat16),
            pltpu.VMEM((2, rows, 1), jnp.float32),
            pltpu.VMEM((2, rows, 128), jnp.float32),
            pltpu.VMEM((2, rows, HEAD_SIZE), jnp.float32),
        ],
        compiler_params=pltpu.CompilerParams(vmem_limit_bytes=40 * 2**20),
    )(info, queries, *key_blocks, *value_blocks)


def z_ring(block):
    planes = lax.axis_size("z")
    blocks = [block] * planes
    upward = planes // 2
    for k in range(1, upward + 1):
        blocks[k] = shifted(blocks[k - 1], "z", 1)
    for k in range(planes - 1, upward, -1):
        blocks[k] = shifted(blocks[(k + 1) % planes], "z", -1)
    return blocks


def x_spread(block):
    return [block] + [shifted(block, X, r) for r in range(1, CHIPS_X)]


def shards(
    hidden,
    queries,
    fresh_kv,
    cache_kv,
    cache_fill,
    out_proj,
    norm_gain,
    router_weight,
    expert_labels,
    gate_proj,
    up_proj,
    down_proj,
):
    planes = lax.axis_size("z")
    z, x = lax.axis_index("z"), lax.axis_index(X)
    pair, column, core = lax.axis_index("xh"), lax.axis_index("xl"), lax.axis_index("core")
    tokens, width = hidden.shape[1:]
    heads_each = planes // 2
    kv_heads = fresh_kv.shape[3] // HEAD_SIZE

    weight_rows = lax.all_gather(out_proj[0], GROUP, axis=0, tiled=True)

    joined = jnp.concatenate([cache_kv[0], fresh_kv[0]], axis=1)
    joined = jnp.moveaxis(
        joined.reshape(2, joined.shape[1], kv_heads, HEAD_SIZE), 2, 0
    )
    own = pick(joined, core)[:, None]
    other = swapped(pick(joined, 1 - core), "core")[:, None]
    chip_kv = in_order(core, own, other, 1)
    key_blocks = z_ring(jnp.stack(x_spread(chip_kv[0])))
    value_blocks = x_spread(jnp.stack(z_ring(chip_kv[1])))

    by_head = queries[0].reshape(tokens, 2, heads_each, 2, 2, HEAD_SIZE)
    by_head = jnp.transpose(by_head, (1, 4, 2, 3, 0, 5)).reshape(
        2, 2, 2 * heads_each, tokens, HEAD_SIZE
    )
    chip_queries = in_order(
        core, pick(by_head, core), swapped(pick(by_head, 1 - core), "core"), 2
    )
    group_queries = in_order(
        column,
        pick(chip_queries, column),
        swapped(pick(chip_queries, 1 - column), "xl"),
        1,
    )
    first = (z * 2 + pair) * (4 * tokens)
    info = jnp.stack([z, x, cache_fill[0], first]).astype(jnp.int32)
    block = min(1024, planes * 8 * (joined.shape[2] - tokens))
    halves = attend(info, group_queries, key_blocks, value_blocks, block)
    features = in_order(core, pick(halves, core), swapped(pick(halves, 1 - core), "core"), 1)
    features = features.reshape(2, 2 * tokens, features.shape[1])

    def projection(side):
        both = jnp.dot(
            pick(features, side), weight_rows, preferred_element_type=jnp.float32
        ).reshape(2, tokens, width)
        return pick(both, core) + swapped(
            pick(both, 1 - core).astype(jnp.bfloat16), "core"
        ).astype(jnp.float32)

    far = swapped(projection(1 - column).astype(jnp.bfloat16), "xl")
    mixed = hidden[0].astype(jnp.float32) + projection(column) + far.astype(jnp.float32)
    inverse = lax.rsqrt(jnp.mean(mixed * mixed, axis=1, keepdims=True) + 1e-06)
    normed = (mixed * inverse * norm_gain[0].astype(jnp.float32)[None, :]).astype(jnp.bfloat16)

    label_rows = expert_labels[0]
    experts = planes * 2
    airborne = label_rows < experts
    chosen = jnp.sum(jnp.where(airborne, label_rows, 0), axis=1)
    capacity = 8
    member = (chosen[:, None] == jnp.arange(experts, dtype=jnp.int32)[None, :]).astype(jnp.int32)
    earlier = jnp.cumsum(member, axis=0) - member
    code = chosen * capacity + jnp.sum(earlier * member, axis=1)
    table = (
        code[None, :] == jnp.arange(experts * capacity, dtype=jnp.int32)[:, None]
    ).astype(jnp.bfloat16)
    packed = jnp.dot(table, normed, preferred_element_type=jnp.float32).astype(jnp.bfloat16)

    logits = jnp.dot(normed, router_weight[0], preferred_element_type=jnp.float32)
    matches = label_rows[:, :, None] == jnp.arange(EXPERTS, dtype=jnp.int32)[None, None, :]
    picked = jnp.sum(jnp.where(matches, logits[:, None, :], 0.0), axis=2)
    probabilities = jax.nn.softmax(picked, axis=1)
    combine = jnp.sum(jnp.where(airborne, probabilities, 0.0), axis=1)

    near_rows = lax.all_to_all(packed, GROUP, split_axis=0, concat_axis=0, tiled=True)
    far_rows = swapped(near_rows, "xl")

    def expert(rows):
        both = jnp.concatenate([rows, swapped(rows, "core")], axis=0)
        gated = jnp.dot(both, gate_proj[0, 0], preferred_element_type=jnp.float32)
        lifted = jnp.dot(both, up_proj[0, 0], preferred_element_type=jnp.float32)
        activation = (jax.nn.silu(gated) * lifted).astype(jnp.bfloat16)
        output = jnp.dot(activation, down_proj[0, 0], preferred_element_type=jnp.float32)
        count = rows.shape[0]
        return output[:count] + swapped(
            output[count:].astype(jnp.bfloat16), "core"
        ).astype(jnp.float32)

    near_sum = expert(near_rows)
    far_sum = swapped(expert(far_rows).astype(jnp.bfloat16), "xl")
    summed = (near_sum + far_sum.astype(jnp.float32)).astype(jnp.bfloat16)
    returned = lax.all_to_all(summed, GROUP, split_axis=0, concat_axis=0, tiled=True)
    routed = lax.dot_general(
        table, returned, (((0,), (0,)), ((), ())), preferred_element_type=jnp.float32
    )
    result = (mixed + combine[:, None] * routed).astype(jnp.bfloat16)
    return shifted(result[None], "section", 1)


def solution(mesh):
    sections, devices = mesh.devices.shape
    planes = devices // (2 * CHIPS_X)
    fine = Mesh(
        mesh.devices.reshape(sections, planes, 2, 2, 2), ("section",) + EXPERT
    )
    in_specs = (
        P("section", EXPERT, None),
        P("section", EXPERT, None),
        P("section", None, EXPERT, None),
        P("section", None, EXPERT, None),
        P("section"),
        P("section", EXPERT, None),
        P("section", None),
        P("section", None, None),
        P("section", EXPERT, None),
        P("section", EXPERT, None, None),
        P("section", EXPERT, None, None),
        P("section", EXPERT, None, None),
    )
    out_specs = P("section", EXPERT, None)
    return jax.shard_map(shards, mesh=fine, in_specs=in_specs, out_specs=out_specs, check_vma=False)
```

```python
import functools
import math

import jax
import jax.numpy as jnp
from jax import lax
from jax.experimental import pallas as pl
from jax.experimental.pallas import tpu as pltpu
from jax.sharding import Mesh
from jax.sharding import PartitionSpec as P

EXPERTS = 128
HEAD_SIZE = 128
SPLIT = 4
CHIPS_X = 4
X = ("xh", "xl")
EXPERT = ("z", "xh", "xl", "core")
GROUP = ("z", "xh")


def shifted(shard, axis, by):
    length = lax.axis_size(axis)
    return lax.ppermute(shard, axis, [(i, (i + by) % length) for i in range(length)])


def swapped(shard, axis):
    return lax.ppermute(shard, axis, [(0, 1), (1, 0)])


def in_order(index, own, other, axis):
    return jnp.where(
        index == 0,
        jnp.concatenate([own, other], axis=axis),
        jnp.concatenate([other, own], axis=axis),
    )


def pick(array, index, axis=0):
    return lax.dynamic_index_in_dim(array, index, axis, keepdims=False)


def attention_kernel(planes, columns, block, info_ref, query_ref, *refs):
    key_blocks = refs[:planes]
    value_blocks = refs[planes : planes + columns]
    out_ref, keys, values, top, total, acc = refs[planes + columns :]
    z, x, fill, first = info_ref[0], info_ref[1], info_ref[2], info_ref[3]
    local = key_blocks[0].shape[2]
    fresh = (2 * local) // 3
    cached = local - fresh
    cache_rows = 2 * planes * columns * cached
    pairs = query_ref.shape[0] // 2
    half = HEAD_SIZE // 2
    for k in range(planes):
        plane = lax.rem(z - k + planes, planes)
        for r in range(columns):
            chip = plane * columns + lax.rem(x - r + columns, columns)
            at_cache = pl.multiple_of(chip * 2 * cached, 2 * cached)
            at_fresh = pl.multiple_of(cache_rows + chip * 2 * fresh, 2 * fresh)
            for held, part in ((keys, key_blocks[k].at[r]), (values, value_blocks[r].at[k])):
                held[pl.ds(at_cache, 2 * cached), :] = part[:, :cached, :].reshape(
                    2 * cached, HEAD_SIZE
                )
                held[pl.ds(at_fresh, 2 * fresh), :] = part[:, cached:, :].reshape(
                    2 * fresh, HEAD_SIZE
                )
    rate = math.log2(math.e) / math.sqrt(HEAD_SIZE)

    def visit(pair, start, visible):
        for u in range(2):
            scores = lax.dot_general(
                query_ref[2 * pair + u],
                keys[pl.ds(start, block), :],
                (((1,), (1,)), ((), ())),
                preferred_element_type=jnp.float32,
            )
            if visible is not None:
                mask = visible(scores.shape)
                scores = jnp.where(mask, scores, -1e30)
            before = top[u]
            high = jnp.maximum(before, jnp.max(scores, axis=1, keepdims=True))
            weights = jnp.exp2((scores - high) * rate)
            if visible is not None:
                weights = jnp.where(mask, weights, 0.0)
            factor = jnp.exp2((before - high) * rate)
            part = weights[:, :128]
            for n in range(1, block // 128):
                part = part + weights[:, n * 128 : (n + 1) * 128]
            total[u] = total[u] * factor + part
            top[u] = high
            acc[u] = acc[u] * factor + jnp.dot(
                weights.astype(jnp.bfloat16),
                values[pl.ds(start, block), :],
                preferred_element_type=jnp.float32,
            )

    def one_pair(pair, unused):
        top[...] = jnp.full_like(top, -1e30)
        total[...] = jnp.zeros_like(total)
        acc[...] = jnp.zeros_like(acc)

        def plain(base):
            def body(n, unused):
                visit(pair, pl.multiple_of(base + n * block, block), None)
                return unused

            return body

        full = fill // block
        lax.fori_loop(0, full, plain(0), 0)

        @pl.when(fill > full * block)
        def _():
            start = pl.multiple_of(full * block, block)
            visit(
                pair,
                start,
                lambda shape: start + lax.broadcasted_iota(jnp.int32, shape, 1) < fill,
            )

        done = first // block
        lax.fori_loop(0, done, plain(cache_rows), 0)
        ahead = done * block - first
        visit(
            pair,
            pl.multiple_of(cache_rows + done * block, block),
            lambda shape: ahead + lax.broadcasted_iota(jnp.int32, shape, 1)
            <= lax.broadcasted_iota(jnp.int32, shape, 0),
        )
        heads = [
            (acc[u] / jnp.sum(total[u], axis=1, keepdims=True)).astype(out_ref.dtype)
            for u in range(2)
        ]
        at = pl.multiple_of(pair * 2 * half, 2 * half)
        for n in range(2):
            out_ref[n, :, pl.ds(at, 2 * half)] = jnp.concatenate(
                [head[:, n * half : (n + 1) * half] for head in heads], axis=1
            )
        return unused

    lax.fori_loop(0, pairs, one_pair, 0)


def attend(info, queries, key_blocks, value_blocks, block):
    planes, columns = len(key_blocks), len(value_blocks)
    heads, rows, unused = queries.shape
    total_rows = planes * columns * 2 * key_blocks[0].shape[2]
    return pl.pallas_call(
        functools.partial(attention_kernel, planes, columns, block),
        out_shape=jax.ShapeDtypeStruct((2, rows, heads * HEAD_SIZE // 2), jnp.bfloat16),
        in_specs=[pl.BlockSpec(memory_space=pltpu.SMEM)]
        + [pl.BlockSpec(memory_space=pltpu.VMEM)] * (1 + planes + columns),
        out_specs=pl.BlockSpec(memory_space=pltpu.VMEM),
        scratch_shapes=[
            pltpu.VMEM((total_rows, HEAD_SIZE), jnp.bfloat16),
            pltpu.VMEM((total_rows, HEAD_SIZE), jnp.bfloat16),
            pltpu.VMEM((2, rows, 1), jnp.float32),
            pltpu.VMEM((2, rows, 128), jnp.float32),
            pltpu.VMEM((2, rows, HEAD_SIZE), jnp.float32),
        ],
        compiler_params=pltpu.CompilerParams(vmem_limit_bytes=40 * 2**20),
    )(info, queries, *key_blocks, *value_blocks)


def z_ring(block):
    planes = lax.axis_size("z")
    blocks = [block] * planes
    upward = planes // 2
    for k in range(1, upward + 1):
        blocks[k] = shifted(blocks[k - 1], "z", 1)
    for k in range(planes - 1, upward, -1):
        blocks[k] = shifted(blocks[(k + 1) % planes], "z", -1)
    return blocks


def x_spread(block):
    return [block] + [shifted(block, X, r) for r in range(1, CHIPS_X)]


def shards(
    hidden,
    queries,
    fresh_kv,
    cache_kv,
    cache_fill,
    out_proj,
    norm_gain,
    router_weight,
    expert_labels,
    gate_proj,
    up_proj,
    down_proj,
):
    planes = lax.axis_size("z")
    z, x = lax.axis_index("z"), lax.axis_index(X)
    core = lax.axis_index("core")
    tokens, width = hidden.shape[1:]
    heads_each = planes // 2
    kv_heads = fresh_kv.shape[3] // HEAD_SIZE

    joined = jnp.concatenate([cache_kv[0], fresh_kv[0]], axis=1)
    joined = jnp.moveaxis(
        joined.reshape(2, joined.shape[1], kv_heads, HEAD_SIZE), 2, 0
    )
    own = pick(joined, core)[:, None]
    other = swapped(pick(joined, 1 - core), "core")[:, None]
    chip_kv = in_order(core, own, other, 1)
    key_blocks = z_ring(jnp.stack(x_spread(chip_kv[0])))
    value_ring = jnp.stack(z_ring(chip_kv[1]))
    own_rows, key_blocks, value_ring = lax.optimization_barrier(
        (out_proj[0], key_blocks, value_ring)
    )
    weight_rows = lax.all_gather(own_rows, "z", axis=0, tiled=True)
    value_blocks = x_spread(value_ring)

    by_head = queries[0].reshape(tokens, 2, heads_each, CHIPS_X, HEAD_SIZE)
    by_head = jnp.transpose(by_head, (1, 3, 2, 0, 4))
    chip_queries = in_order(
        core, pick(by_head, core), swapped(pick(by_head, 1 - core), "core"), 2
    )
    from_column = [pick(chip_queries, x)] + [
        shifted(pick(chip_queries, (x + r) % CHIPS_X), X, r) for r in range(1, CHIPS_X)
    ]
    group_queries = jnp.stack(from_column, axis=1)
    group_queries = jnp.concatenate(
        [pick(group_queries, (x - n) % CHIPS_X, 1) for n in range(CHIPS_X)], axis=1
    )
    first = z * (2 * CHIPS_X * tokens)
    info = jnp.stack([z, x, cache_fill[0], first]).astype(jnp.int32)
    block = min(1024, planes * 8 * (joined.shape[2] - tokens))
    halves = attend(info, group_queries, key_blocks, value_blocks, block)
    features = in_order(core, pick(halves, core), swapped(pick(halves, 1 - core), "core"), 1)
    features = features.reshape(CHIPS_X, 2 * tokens, features.shape[1])

    def projection(step):
        both = jnp.dot(
            pick(features, (x + step) % CHIPS_X), weight_rows, preferred_element_type=jnp.float32
        ).reshape(2, tokens, width)
        return pick(both, core) + swapped(
            pick(both, 1 - core).astype(jnp.bfloat16), "core"
        ).astype(jnp.float32)

    def sent(part, by):
        return shifted(part.astype(jnp.bfloat16), X, by).astype(jnp.float32)

    middle = width // 2
    opposite = projection(2)
    relay_up, relay_down = sent(opposite[:, :middle], 1), sent(opposite[:, middle:], -1)
    above, below = projection(1), projection(3)
    low = sent(below[:, :middle], -1) + sent(above[:, :middle] + relay_up, 1)
    high = sent(above[:, middle:], 1) + sent(below[:, middle:] + relay_down, -1)
    mixed = (
        hidden[0].astype(jnp.float32) + projection(0) + jnp.concatenate([low, high], axis=1)
    )
    inverse = lax.rsqrt(jnp.mean(mixed * mixed, axis=1, keepdims=True) + 1e-06)
    normed = (mixed * inverse * norm_gain[0].astype(jnp.float32)[None, :]).astype(jnp.bfloat16)

    label_rows = expert_labels[0]
    experts = planes * 2
    airborne = label_rows < experts
    chosen = jnp.sum(jnp.where(airborne, label_rows, 0), axis=1)
    capacity = 8
    member = (chosen[:, None] == jnp.arange(experts, dtype=jnp.int32)[None, :]).astype(jnp.int32)
    earlier = jnp.cumsum(member, axis=0) - member
    code = chosen * capacity + jnp.sum(earlier * member, axis=1)
    table = (
        code[None, :] == jnp.arange(experts * capacity, dtype=jnp.int32)[:, None]
    ).astype(jnp.bfloat16)
    packed = jnp.dot(table, normed, preferred_element_type=jnp.float32).astype(jnp.bfloat16)

    logits = jnp.dot(normed, router_weight[0], preferred_element_type=jnp.float32)
    matches = label_rows[:, :, None] == jnp.arange(EXPERTS, dtype=jnp.int32)[None, None, :]
    picked = jnp.sum(jnp.where(matches, logits[:, None, :], 0.0), axis=2)
    probabilities = jax.nn.softmax(picked, axis=1)
    combine = jnp.sum(jnp.where(airborne, probabilities, 0.0), axis=1)

    near_rows = lax.all_to_all(packed, GROUP, split_axis=0, concat_axis=0, tiled=True)
    far_rows = swapped(near_rows, "xl")

    def expert(rows):
        both = jnp.concatenate([rows, swapped(rows, "core")], axis=0)
        gated = jnp.dot(both, gate_proj[0, 0], preferred_element_type=jnp.float32)
        lifted = jnp.dot(both, up_proj[0, 0], preferred_element_type=jnp.float32)
        activation = (jax.nn.silu(gated) * lifted).astype(jnp.bfloat16)
        output = jnp.dot(activation, down_proj[0, 0], preferred_element_type=jnp.float32)
        count = rows.shape[0]
        return output[:count] + swapped(
            output[count:].astype(jnp.bfloat16), "core"
        ).astype(jnp.float32)

    near_sum = expert(near_rows)
    far_sum = swapped(expert(far_rows).astype(jnp.bfloat16), "xl")
    summed = (near_sum + far_sum.astype(jnp.float32)).astype(jnp.bfloat16)
    returned = lax.all_to_all(summed, GROUP, split_axis=0, concat_axis=0, tiled=True)
    routed = lax.dot_general(
        table, returned, (((0,), (0,)), ((), ())), preferred_element_type=jnp.float32
    )
    result = (mixed + combine[:, None] * routed).astype(jnp.bfloat16)
    return shifted(result[None], "section", 1)


def solution(mesh):
    sections, devices = mesh.devices.shape
    planes = devices // (2 * CHIPS_X)
    fine = Mesh(
        mesh.devices.reshape(sections, planes, 2, 2, 2), ("section",) + EXPERT
    )
    in_specs = (
        P("section", EXPERT, None),
        P("section", EXPERT, None),
        P("section", None, EXPERT, None),
        P("section", None, EXPERT, None),
        P("section"),
        P("section", EXPERT, None),
        P("section", None),
        P("section", None, None),
        P("section", EXPERT, None),
        P("section", EXPERT, None, None),
        P("section", EXPERT, None, None),
        P("section", EXPERT, None, None),
    )
    out_specs = P("section", EXPERT, None)
    return jax.shard_map(shards, mesh=fine, in_specs=in_specs, out_specs=out_specs, check_vma=False)
```

```python
import functools
import math

import jax
import jax.numpy as jnp
from jax import lax
from jax.experimental import pallas as pl
from jax.experimental.pallas import tpu as pltpu
from jax.sharding import Mesh
from jax.sharding import PartitionSpec as P

EXPERTS = 128
HEAD_SIZE = 128
SPLIT = 4
CHIPS_X = 4
X = ("xh", "xl")
EXPERT = ("z", "xh", "xl", "core")
GROUP = ("z", "xh")


def shifted(shard, axis, by):
    length = lax.axis_size(axis)
    return lax.ppermute(shard, axis, [(i, (i + by) % length) for i in range(length)])


def swapped(shard, axis):
    return lax.ppermute(shard, axis, [(0, 1), (1, 0)])


def in_order(index, own, other, axis):
    return jnp.where(
        index == 0,
        jnp.concatenate([own, other], axis=axis),
        jnp.concatenate([other, own], axis=axis),
    )


def pick(array, index, axis=0):
    return lax.dynamic_index_in_dim(array, index, axis, keepdims=False)


def attention_kernel(planes, columns, block, info_ref, query_ref, *refs):
    key_blocks = refs[:planes]
    value_blocks = refs[planes : planes + columns]
    out_ref, keys, values, top, total, acc = refs[planes + columns :]
    z, x, fill, first = info_ref[0], info_ref[1], info_ref[2], info_ref[3]
    local = key_blocks[0].shape[2]
    fresh = (2 * local) // 3
    cached = local - fresh
    cache_rows = 2 * planes * columns * cached
    pairs = query_ref.shape[0] // 2
    half = HEAD_SIZE // 2
    for k in range(planes):
        plane = lax.rem(z - k + planes, planes)
        for r in range(columns):
            chip = plane * columns + lax.rem(x - r + columns, columns)
            at_cache = pl.multiple_of(chip * 2 * cached, 2 * cached)
            at_fresh = pl.multiple_of(cache_rows + chip * 2 * fresh, 2 * fresh)
            for held, part in ((keys, key_blocks[k].at[r]), (values, value_blocks[r].at[k])):
                held[pl.ds(at_cache, 2 * cached), :] = part[:, :cached, :].reshape(
                    2 * cached, HEAD_SIZE
                )
                held[pl.ds(at_fresh, 2 * fresh), :] = part[:, cached:, :].reshape(
                    2 * fresh, HEAD_SIZE
                )
    rate = math.log2(math.e) / math.sqrt(HEAD_SIZE)

    def visit(pair, start, visible):
        for u in range(2):
            scores = lax.dot_general(
                query_ref[2 * pair + u],
                keys[pl.ds(start, block), :],
                (((1,), (1,)), ((), ())),
                preferred_element_type=jnp.float32,
            )
            if visible is not None:
                mask = visible(scores.shape)
                scores = jnp.where(mask, scores, -1e30)
            before = top[u]
            high = jnp.maximum(before, jnp.max(scores, axis=1, keepdims=True))
            weights = jnp.exp2((scores - high) * rate)
            if visible is not None:
                weights = jnp.where(mask, weights, 0.0)
            factor = jnp.exp2((before - high) * rate)
            part = weights[:, :128]
            for n in range(1, block // 128):
                part = part + weights[:, n * 128 : (n + 1) * 128]
            total[u] = total[u] * factor + part
            top[u] = high
            acc[u] = acc[u] * factor + jnp.dot(
                weights.astype(jnp.bfloat16),
                values[pl.ds(start, block), :],
                preferred_element_type=jnp.float32,
            )

    def one_pair(pair, unused):
        top[...] = jnp.full_like(top, -1e30)
        total[...] = jnp.zeros_like(total)
        acc[...] = jnp.zeros_like(acc)

        def plain(base):
            def body(n, unused):
                visit(pair, pl.multiple_of(base + n * block, block), None)
                return unused

            return body

        full = fill // block
        lax.fori_loop(0, full, plain(0), 0)

        @pl.when(fill > full * block)
        def _():
            start = pl.multiple_of(full * block, block)
            visit(
                pair,
                start,
                lambda shape: start + lax.broadcasted_iota(jnp.int32, shape, 1) < fill,
            )

        done = first // block
        lax.fori_loop(0, done, plain(cache_rows), 0)
        ahead = done * block - first
        visit(
            pair,
            pl.multiple_of(cache_rows + done * block, block),
            lambda shape: ahead + lax.broadcasted_iota(jnp.int32, shape, 1)
            <= lax.broadcasted_iota(jnp.int32, shape, 0),
        )
        heads = [
            (acc[u] / jnp.sum(total[u], axis=1, keepdims=True)).astype(out_ref.dtype)
            for u in range(2)
        ]
        at = pl.multiple_of(pair * 2 * half, 2 * half)
        for n in range(2):
            out_ref[n, :, pl.ds(at, 2 * half)] = jnp.concatenate(
                [head[:, n * half : (n + 1) * half] for head in heads], axis=1
            )
        return unused

    lax.fori_loop(0, pairs, one_pair, 0)


def attend(info, queries, key_blocks, value_blocks, block):
    planes, columns = len(key_blocks), len(value_blocks)
    heads, rows, unused = queries.shape
    total_rows = planes * columns * 2 * key_blocks[0].shape[2]
    return pl.pallas_call(
        functools.partial(attention_kernel, planes, columns, block),
        out_shape=jax.ShapeDtypeStruct((2, rows, heads * HEAD_SIZE // 2), jnp.bfloat16),
        in_specs=[pl.BlockSpec(memory_space=pltpu.SMEM)]
        + [pl.BlockSpec(memory_space=pltpu.VMEM)] * (1 + planes + columns),
        out_specs=pl.BlockSpec(memory_space=pltpu.VMEM),
        scratch_shapes=[
            pltpu.VMEM((total_rows, HEAD_SIZE), jnp.bfloat16),
            pltpu.VMEM((total_rows, HEAD_SIZE), jnp.bfloat16),
            pltpu.VMEM((2, rows, 1), jnp.float32),
            pltpu.VMEM((2, rows, 128), jnp.float32),
            pltpu.VMEM((2, rows, HEAD_SIZE), jnp.float32),
        ],
        compiler_params=pltpu.CompilerParams(vmem_limit_bytes=40 * 2**20),
    )(info, queries, *key_blocks, *value_blocks)


def z_ring(block, beside=None):
    planes = lax.axis_size("z")
    blocks = [block] * planes
    upward = planes // 2
    for k in range(1, upward + 1):
        blocks[k] = shifted(blocks[k - 1], "z", 1)
        if k == 2 and beside is not None:
            blocks[k], beside = lax.optimization_barrier((blocks[k], beside))
    for k in range(planes - 1, upward, -1):
        blocks[k] = shifted(blocks[(k + 1) % planes], "z", -1)
    return blocks, beside


def x_spread(block):
    return [block] + [shifted(block, X, r) for r in range(1, CHIPS_X)]


def shards(
    hidden,
    queries,
    fresh_kv,
    cache_kv,
    cache_fill,
    out_proj,
    norm_gain,
    router_weight,
    expert_labels,
    gate_proj,
    up_proj,
    down_proj,
):
    planes = lax.axis_size("z")
    z, x = lax.axis_index("z"), lax.axis_index(X)
    core = lax.axis_index("core")
    tokens, width = hidden.shape[1:]
    heads_each = planes // 2
    kv_heads = fresh_kv.shape[3] // HEAD_SIZE

    joined = jnp.concatenate([cache_kv[0], fresh_kv[0]], axis=1)
    joined = jnp.moveaxis(
        joined.reshape(2, joined.shape[1], kv_heads, HEAD_SIZE), 2, 0
    )
    own = pick(joined, core)[:, None]
    other = swapped(pick(joined, 1 - core), "core")[:, None]
    chip_kv = in_order(core, own, other, 1)
    by_head = queries[0].reshape(tokens, 2, heads_each, CHIPS_X, HEAD_SIZE)
    by_head = jnp.transpose(by_head, (1, 3, 2, 0, 4))
    chip_queries = in_order(
        core, pick(by_head, core), swapped(pick(by_head, 1 - core), "core"), 2
    )
    from_column = [pick(chip_queries, x)] + [
        shifted(pick(chip_queries, (x + r) % CHIPS_X), X, r) for r in range(1, CHIPS_X)
    ]
    group_queries = jnp.stack(from_column, axis=1)
    group_queries = jnp.concatenate(
        [pick(group_queries, (x - n) % CHIPS_X, 1) for n in range(CHIPS_X)], axis=1
    )
    key_blocks, group_queries = z_ring(jnp.stack(x_spread(chip_kv[0])), group_queries)
    own_rows, key_blocks = lax.optimization_barrier((out_proj[0], key_blocks))
    weight_rows = lax.all_gather(own_rows, "z", axis=0, tiled=True)
    value_blocks = x_spread(jnp.stack(z_ring(chip_kv[1])[0]))
    first = z * (2 * CHIPS_X * tokens)
    info = jnp.stack([z, x, cache_fill[0], first]).astype(jnp.int32)
    block = min(1024, planes * 8 * (joined.shape[2] - tokens))
    halves = attend(info, group_queries, key_blocks, value_blocks, block)
    features = in_order(core, pick(halves, core), swapped(pick(halves, 1 - core), "core"), 1)
    features = features.reshape(CHIPS_X, 2 * tokens, features.shape[1])

    def projection(step):
        both = jnp.dot(
            pick(features, (x + step) % CHIPS_X), weight_rows, preferred_element_type=jnp.float32
        ).reshape(2, tokens, width)
        return pick(both, core) + swapped(
            pick(both, 1 - core).astype(jnp.bfloat16), "core"
        ).astype(jnp.float32)

    def sent(part, by):
        return shifted(part.astype(jnp.bfloat16), X, by).astype(jnp.float32)

    middle = width // 2
    opposite = projection(2)
    relay_up, relay_down = sent(opposite[:, :middle], 1), sent(opposite[:, middle:], -1)
    above, below = projection(1), projection(3)
    low = sent(below[:, :middle], -1) + sent(above[:, :middle] + relay_up, 1)
    high = sent(above[:, middle:], 1) + sent(below[:, middle:] + relay_down, -1)
    mixed = (
        hidden[0].astype(jnp.float32) + projection(0) + jnp.concatenate([low, high], axis=1)
    )
    inverse = lax.rsqrt(jnp.mean(mixed * mixed, axis=1, keepdims=True) + 1e-06)
    normed = (mixed * inverse * norm_gain[0].astype(jnp.float32)[None, :]).astype(jnp.bfloat16)

    label_rows = expert_labels[0]
    experts = planes * 2
    airborne = label_rows < experts
    chosen = jnp.sum(jnp.where(airborne, label_rows, 0), axis=1)
    capacity = 8
    member = (chosen[:, None] == jnp.arange(experts, dtype=jnp.int32)[None, :]).astype(jnp.int32)
    earlier = jnp.cumsum(member, axis=0) - member
    code = chosen * capacity + jnp.sum(earlier * member, axis=1)
    table = (
        code[None, :] == jnp.arange(experts * capacity, dtype=jnp.int32)[:, None]
    ).astype(jnp.bfloat16)
    packed = jnp.dot(table, normed, preferred_element_type=jnp.float32).astype(jnp.bfloat16)

    logits = jnp.dot(normed, router_weight[0], preferred_element_type=jnp.float32)
    matches = label_rows[:, :, None] == jnp.arange(EXPERTS, dtype=jnp.int32)[None, None, :]
    picked = jnp.sum(jnp.where(matches, logits[:, None, :], 0.0), axis=2)
    probabilities = jax.nn.softmax(picked, axis=1)
    combine = jnp.sum(jnp.where(airborne, probabilities, 0.0), axis=1)

    near_rows = lax.all_to_all(packed, GROUP, split_axis=0, concat_axis=0, tiled=True)
    far_rows = swapped(near_rows, "xl")

    def expert(rows):
        both = jnp.concatenate([rows, swapped(rows, "core")], axis=0)
        gated = jnp.dot(both, gate_proj[0, 0], preferred_element_type=jnp.float32)
        lifted = jnp.dot(both, up_proj[0, 0], preferred_element_type=jnp.float32)
        activation = (jax.nn.silu(gated) * lifted).astype(jnp.bfloat16)
        output = jnp.dot(activation, down_proj[0, 0], preferred_element_type=jnp.float32)
        count = rows.shape[0]
        return output[:count] + swapped(
            output[count:].astype(jnp.bfloat16), "core"
        ).astype(jnp.float32)

    near_sum = expert(near_rows)
    near_sum, far_rows = lax.optimization_barrier((near_sum, far_rows))
    far_sum = swapped(expert(far_rows).astype(jnp.bfloat16), "xl")
    summed = (near_sum + far_sum.astype(jnp.float32)).astype(jnp.bfloat16)
    returned = lax.all_to_all(summed, GROUP, split_axis=0, concat_axis=0, tiled=True)
    routed = lax.dot_general(
        table, returned, (((0,), (0,)), ((), ())), preferred_element_type=jnp.float32
    )
    result = (mixed + combine[:, None] * routed).astype(jnp.bfloat16)
    return shifted(result[None], "section", 1)


def solution(mesh):
    sections, devices = mesh.devices.shape
    planes = devices // (2 * CHIPS_X)
    fine = Mesh(
        mesh.devices.reshape(sections, planes, 2, 2, 2), ("section",) + EXPERT
    )
    in_specs = (
        P("section", EXPERT, None),
        P("section", EXPERT, None),
        P("section", None, EXPERT, None),
        P("section", None, EXPERT, None),
        P("section"),
        P("section", EXPERT, None),
        P("section", None),
        P("section", None, None),
        P("section", EXPERT, None),
        P("section", EXPERT, None, None),
        P("section", EXPERT, None, None),
        P("section", EXPERT, None, None),
    )
    out_specs = P("section", EXPERT, None)
    return jax.shard_map(shards, mesh=fine, in_specs=in_specs, out_specs=out_specs, check_vma=False)
```

```python
import functools
import math

import jax
import jax.numpy as jnp
from jax import lax
from jax.experimental import pallas as pl
from jax.experimental.pallas import tpu as pltpu
from jax.sharding import Mesh
from jax.sharding import PartitionSpec as P

EXPERTS = 128
HEAD_SIZE = 128
SPLIT = 4
CHIPS_X = 4
X = ("xh", "xl")
EXPERT = ("z", "xh", "xl", "core")
GROUP = ("z", "xh")


def shifted(shard, axis, by):
    length = lax.axis_size(axis)
    return lax.ppermute(shard, axis, [(i, (i + by) % length) for i in range(length)])


def swapped(shard, axis):
    return lax.ppermute(shard, axis, [(0, 1), (1, 0)])


def in_order(index, own, other, axis):
    return jnp.where(
        index == 0,
        jnp.concatenate([own, other], axis=axis),
        jnp.concatenate([other, own], axis=axis),
    )


def pick(array, index, axis=0):
    return lax.dynamic_index_in_dim(array, index, axis, keepdims=False)


def joining_kernel(count, *refs):
    parts, out_ref, semaphores = refs[:count], refs[count], refs[count + 1]
    copies = [
        pltpu.make_async_copy(part, out_ref.at[n], semaphores.at[n])
        for n, part in enumerate(parts)
    ]
    for copy in copies:
        copy.start()
    for copy in copies:
        copy.wait()


def joined_blocks(blocks):
    count = len(blocks)
    return pl.pallas_call(
        functools.partial(joining_kernel, count),
        out_shape=jax.ShapeDtypeStruct((count,) + blocks[0].shape, blocks[0].dtype),
        in_specs=[pl.BlockSpec(memory_space=pl.ANY)] * count,
        out_specs=pl.BlockSpec(memory_space=pl.ANY),
        scratch_shapes=[pltpu.SemaphoreType.DMA((count,))],
    )(*blocks)


def attention_kernel(planes, columns, block, info_ref, *refs):
    query_blocks = refs[:columns]
    key_blocks = refs[columns : columns + planes]
    value_blocks = refs[columns + planes : 2 * columns + planes]
    keep_ref, send_ref, query_ref, keys, values, top, total, acc = refs[2 * columns + planes :]
    z, x, core, fill = info_ref[0], info_ref[1], info_ref[2], info_ref[3]
    local = key_blocks[0].shape[2]
    fresh = (2 * local) // 3
    cached = local - fresh
    cache_rows = 2 * planes * columns * cached
    heads = query_ref.shape[0]
    half = HEAD_SIZE // 2
    first = z * (2 * columns * fresh)
    for r in range(columns):
        from_x = lax.rem(x - r + columns, columns)
        for n in range(2):
            from_core = core if n == 0 else 1 - core
            at = pl.multiple_of((from_x * 2 + from_core) * fresh, fresh)
            for head in range(heads):
                query_ref[head, pl.ds(at, fresh), :] = query_blocks[r][
                    n * fresh : (n + 1) * fresh, head * HEAD_SIZE : (head + 1) * HEAD_SIZE
                ]
    for k in range(planes):
        plane = lax.rem(z - k + planes, planes)
        for r in range(columns):
            chip = plane * columns + lax.rem(x - r + columns, columns)
            for n in range(2):
                device = chip * 2 + (core if n == 0 else 1 - core)
                at_cache = pl.multiple_of(device * cached, cached)
                at_fresh = pl.multiple_of(cache_rows + device * fresh, fresh)
                for held, part in ((keys, key_blocks[k]), (values, value_blocks[r])):
                    where = (r, n) if held is keys else (k, n)
                    held[pl.ds(at_cache, cached), :] = part[where[0], where[1], :cached, :]
                    held[pl.ds(at_fresh, fresh), :] = part[where[0], where[1], cached:, :]
    rate = math.log2(math.e) / math.sqrt(HEAD_SIZE)

    def visit(pair, start, visible):
        for u in range(2):
            scores = lax.dot_general(
                query_ref[2 * pair + u],
                keys[pl.ds(start, block), :],
                (((1,), (1,)), ((), ())),
                preferred_element_type=jnp.float32,
            )
            if visible is not None:
                mask = visible(scores.shape)
                scores = jnp.where(mask, scores, -1e30)
            before = top[u]
            high = jnp.maximum(before, jnp.max(scores, axis=1, keepdims=True))
            weights = jnp.exp2((scores - high) * rate)
            if visible is not None:
                weights = jnp.where(mask, weights, 0.0)
            factor = jnp.exp2((before - high) * rate)
            part = weights[:, :128]
            for n in range(1, block // 128):
                part = part + weights[:, n * 128 : (n + 1) * 128]
            total[u] = total[u] * factor + part
            top[u] = high
            acc[u] = acc[u] * factor + jnp.dot(
                weights.astype(jnp.bfloat16),
                values[pl.ds(start, block), :],
                preferred_element_type=jnp.float32,
            )

    def one_pair(pair, unused):
        top[...] = jnp.full_like(top, -1e30)
        total[...] = jnp.zeros_like(total)
        acc[...] = jnp.zeros_like(acc)

        def plain(base):
            def body(n, unused):
                visit(pair, pl.multiple_of(base + n * block, block), None)
                return unused

            return body

        full = fill // block
        lax.fori_loop(0, full, plain(0), 0)

        @pl.when(fill > full * block)
        def _():
            start = pl.multiple_of(full * block, block)
            visit(
                pair,
                start,
                lambda shape: start + lax.broadcasted_iota(jnp.int32, shape, 1) < fill,
            )

        done = first // block
        lax.fori_loop(0, done, plain(cache_rows), 0)
        ahead = done * block - first
        visit(
            pair,
            pl.multiple_of(cache_rows + done * block, block),
            lambda shape: ahead + lax.broadcasted_iota(jnp.int32, shape, 1)
            <= lax.broadcasted_iota(jnp.int32, shape, 0),
        )
        heads = [acc[u] / jnp.sum(total[u], axis=1, keepdims=True) for u in range(2)]
        at = pl.multiple_of(pair * 2 * half, 2 * half)
        low = jnp.concatenate([head[:, :half] for head in heads], axis=1)
        high = jnp.concatenate([head[:, half:] for head in heads], axis=1)
        keep_ref[:, pl.ds(at, 2 * half)] = jnp.where(core == 0, low, high).astype(keep_ref.dtype)
        send_ref[:, pl.ds(at, 2 * half)] = jnp.where(core == 0, high, low).astype(send_ref.dtype)
        return unused

    lax.fori_loop(0, heads // 2, one_pair, 0)


def attend(info, query_blocks, key_blocks, value_blocks, block):
    planes, columns = len(key_blocks), len(value_blocks)
    chip_rows, features = query_blocks[0].shape
    rows, heads = columns * chip_rows, features // HEAD_SIZE
    total_rows = planes * columns * 2 * key_blocks[0].shape[2]
    out = jax.ShapeDtypeStruct((rows, features // 2), jnp.bfloat16)
    return pl.pallas_call(
        functools.partial(attention_kernel, planes, columns, block),
        out_shape=(out, out),
        in_specs=[pl.BlockSpec(memory_space=pltpu.SMEM)]
        + [pl.BlockSpec()] * (2 * columns + planes),
        out_specs=(pl.BlockSpec(), pl.BlockSpec()),
        scratch_shapes=[
            pltpu.VMEM((heads, rows, HEAD_SIZE), jnp.bfloat16),
            pltpu.VMEM((total_rows, HEAD_SIZE), jnp.bfloat16),
            pltpu.VMEM((total_rows, HEAD_SIZE), jnp.bfloat16),
            pltpu.VMEM((2, rows, 1), jnp.float32),
            pltpu.VMEM((2, rows, 128), jnp.float32),
            pltpu.VMEM((2, rows, HEAD_SIZE), jnp.float32),
        ],
        compiler_params=pltpu.CompilerParams(vmem_limit_bytes=48 * 2**20),
    )(info, *query_blocks, *key_blocks, *value_blocks)


def expert_kernel(steps, *refs):
    rows, (gate_ref, up_ref, down_ref) = refs[:4], refs[4:7]
    keep_ref, send_ref, gated, lifted, activation = refs[7:]
    step = pl.program_id(0)
    count = rows[0].shape[0]
    half = steps // 2

    @pl.when(step == 0)
    def _():
        gated[...] = jnp.zeros_like(gated)
        lifted[...] = jnp.zeros_like(lifted)

    for n in range(2):

        @pl.when((step >= n * half) & (step < (n + 1) * half))
        def _():
            both = jnp.concatenate([rows[2 * n][...], rows[2 * n + 1][...]], axis=0)
            gated[...] += jnp.dot(both, gate_ref[...], preferred_element_type=jnp.float32)
            lifted[...] += jnp.dot(both, up_ref[...], preferred_element_type=jnp.float32)

    @pl.when(step == steps - 1)
    def _():
        activation[...] = (jax.nn.silu(gated[...]) * lifted[...]).astype(activation.dtype)

    @pl.when(step >= steps)
    def _():
        output = jnp.dot(activation[...], down_ref[...], preferred_element_type=jnp.float32)
        keep_ref[...] = output[:count].astype(keep_ref.dtype)
        send_ref[...] = output[count:].astype(send_ref.dtype)


def expert(own, other, gate, up, down):
    count, half_width = own[0].shape
    width, hidden_units = gate.shape
    steps = 4
    part = width // steps

    def row_spec(n):
        return pl.BlockSpec(
            (count, part), lambda i: (0, jnp.clip(i - n * (steps // 2), 0, steps // 2 - 1))
        )

    weight_spec = pl.BlockSpec((part, hidden_units), lambda i: (jnp.minimum(i, steps - 1), 0))
    tail = lambda i: (0, jnp.maximum(i - steps, 0))
    out = jax.ShapeDtypeStruct((count, width), jnp.bfloat16)
    return pl.pallas_call(
        functools.partial(expert_kernel, steps),
        grid=(2 * steps,),
        out_shape=(out, out),
        in_specs=[row_spec(0), row_spec(0), row_spec(1), row_spec(1)]
        + [weight_spec, weight_spec, pl.BlockSpec((hidden_units, part), tail)],
        out_specs=(pl.BlockSpec((count, part), tail), pl.BlockSpec((count, part), tail)),
        scratch_shapes=[
            pltpu.VMEM((2 * count, hidden_units), jnp.float32),
            pltpu.VMEM((2 * count, hidden_units), jnp.float32),
            pltpu.VMEM((2 * count, hidden_units), jnp.bfloat16),
        ],
        compiler_params=pltpu.CompilerParams(vmem_limit_bytes=40 * 2**20),
        cost_estimate=pl.CostEstimate(
            flops=12 * count * width * hidden_units,
            bytes_accessed=6 * width * hidden_units + 8 * count * width,
            transcendentals=2 * count * hidden_units,
        ),
    )(own[0], other[0], own[1], other[1], gate, up, down)


def x_spread(block):
    return [block] + [shifted(block, X, r) for r in range(1, CHIPS_X)]


def shards(
    hidden,
    queries,
    fresh_kv,
    cache_kv,
    cache_fill,
    out_proj,
    norm_gain,
    router_weight,
    expert_labels,
    gate_proj,
    up_proj,
    down_proj,
):
    planes = lax.axis_size("z")
    z, x = lax.axis_index("z"), lax.axis_index(X)
    core = lax.axis_index("core")
    tokens, width = hidden.shape[1:]
    heads_each = planes // 2
    middle = width // 2
    kv_heads = fresh_kv.shape[3] // HEAD_SIZE

    columns = [(x + r) % CHIPS_X for r in range(CHIPS_X)]
    joined = jnp.concatenate([cache_kv[0], fresh_kv[0]], axis=1)
    joined = jnp.moveaxis(
        joined.reshape(2, joined.shape[1], kv_heads, HEAD_SIZE), 2, 0
    )
    own_kv, own_queries = pick(joined, core), pick(queries[0].reshape(tokens, 2, -1), core, 1)
    other_kv = swapped(pick(joined, 1 - core), "core")
    other_queries = swapped(pick(queries[0].reshape(tokens, 2, -1), 1 - core, 1), "core")
    chip_kv = jnp.stack([own_kv, other_kv], axis=1)
    chip_queries = jnp.concatenate([own_queries, other_queries], axis=0).reshape(
        2 * tokens, heads_each, CHIPS_X, HEAD_SIZE
    )
    key_column = x_spread(chip_kv[0])
    value_planes = [chip_kv[1]] + [shifted(chip_kv[1], "z", k) for k in range(1, planes)]
    key_column, value_planes, own_rows, chip_queries = lax.optimization_barrier(
        (key_column, value_planes, out_proj[0], chip_queries)
    )
    weight_rows = lax.all_gather(own_rows, "z", axis=0, tiled=True)
    value_plane = joined_blocks(value_planes)
    value_blocks = x_spread(value_plane)
    query_blocks = [pick(chip_queries, x, 2).reshape(2 * tokens, -1)] + [
        shifted(pick(chip_queries, columns[r], 2).reshape(2 * tokens, -1), X, r)
        for r in range(1, CHIPS_X)
    ]
    key_blocks = [joined_blocks(key_column)] * planes
    upward = planes // 2
    for k in range(1, upward + 1):
        key_blocks[k] = shifted(key_blocks[k - 1], "z", 1)
        if k < planes - k:
            key_blocks[planes - k] = shifted(key_blocks[(planes - k + 1) % planes], "z", -1)
        if k == 2:
            key_blocks, value_blocks[1], value_blocks[3], query_blocks = lax.optimization_barrier(
                (key_blocks, value_blocks[1], value_blocks[3], query_blocks)
            )
    info = jnp.stack([z, x, core, cache_fill[0]]).astype(jnp.int32)
    block = min(1024, planes * 8 * (joined.shape[2] - tokens))
    keep, send = attend(info, query_blocks, key_blocks, value_blocks, block)
    features = in_order(core, keep, swapped(send, "core"), 1)
    features = features.reshape(CHIPS_X, 2 * tokens, features.shape[1])

    def projection(step):
        both = jnp.dot(
            pick(features, (x + step) % CHIPS_X), weight_rows, preferred_element_type=jnp.float32
        ).reshape(2, tokens, width)
        return pick(both, core) + swapped(
            pick(both, 1 - core).astype(jnp.bfloat16), "core"
        ).astype(jnp.float32)

    def sent(part, by):
        return shifted(part.astype(jnp.bfloat16), X, by).astype(jnp.float32)

    opposite = projection(2)
    relay_up, relay_down = sent(opposite[:, :middle], 1), sent(opposite[:, middle:], -1)
    above, below = projection(1), projection(3)
    low = sent(below[:, :middle], -1) + sent(above[:, :middle] + relay_up, 1)
    high = sent(above[:, middle:], 1) + sent(below[:, middle:] + relay_down, -1)
    mixed = (
        hidden[0].astype(jnp.float32) + projection(0) + jnp.concatenate([low, high], axis=1)
    )
    inverse = lax.rsqrt(jnp.mean(mixed * mixed, axis=1, keepdims=True) + 1e-06)
    normed = (mixed * inverse * norm_gain[0].astype(jnp.float32)[None, :]).astype(jnp.bfloat16)

    label_rows = expert_labels[0]
    experts = planes * 2
    airborne = label_rows < experts
    chosen = jnp.sum(jnp.where(airborne, label_rows, 0), axis=1)
    capacity = 8
    member = (chosen[:, None] == jnp.arange(experts, dtype=jnp.int32)[None, :]).astype(jnp.int32)
    earlier = jnp.cumsum(member, axis=0) - member
    code = chosen * capacity + jnp.sum(earlier * member, axis=1)
    table = (
        code[None, :] == jnp.arange(experts * capacity, dtype=jnp.int32)[:, None]
    ).astype(jnp.bfloat16)
    packed = jnp.dot(table, normed, preferred_element_type=jnp.float32).astype(jnp.bfloat16)

    logits = jnp.dot(normed, router_weight[0], preferred_element_type=jnp.float32)
    matches = label_rows[:, :, None] == jnp.arange(EXPERTS, dtype=jnp.int32)[None, None, :]
    picked = jnp.sum(jnp.where(matches, logits[:, None, :], 0.0), axis=2)
    probabilities = jax.nn.softmax(picked, axis=1)
    combine = jnp.sum(jnp.where(airborne, probabilities, 0.0), axis=1)

    parts = (slice(0, middle), slice(middle, width))
    near, near_other, far = [], [], []
    for part in parts:
        rows = lax.all_to_all(packed[:, part], GROUP, split_axis=0, concat_axis=0, tiled=True)
        rows_other = swapped(rows, "core")
        near.append(rows)
        near_other.append(rows_other)
        far.append(swapped(rows, "xl"))
    weights = (gate_proj[0, 0], up_proj[0, 0], down_proj[0, 0])
    near_keep, near_send = expert(near, near_other, *weights)
    far_other = [swapped(rows, "core") for rows in far]
    far_keep, far_send = expert(far, far_other, *weights)

    def wide(array):
        return array.astype(jnp.float32)

    far_sum = (wide(far_keep) + wide(swapped(far_send, "core"))).astype(jnp.bfloat16)
    near_sum = wide(near_keep) + wide(swapped(near_send, "core"))
    finished = []
    for part in parts:
        back = swapped(far_sum[:, part], "xl")
        summed = (near_sum[:, part] + wide(back)).astype(jnp.bfloat16)
        returned = lax.all_to_all(summed, GROUP, split_axis=0, concat_axis=0, tiled=True)
        routed = lax.dot_general(
            table, returned, (((0,), (0,)), ((), ())), preferred_element_type=jnp.float32
        )
        result = (mixed[:, part] + combine[:, None] * routed).astype(jnp.bfloat16)
        finished.append(shifted(result, "section", 1))
    return jnp.concatenate(finished, axis=1)[None]


def solution(mesh):
    sections, devices = mesh.devices.shape
    planes = devices // (2 * CHIPS_X)
    fine = Mesh(
        mesh.devices.reshape(sections, planes, 2, 2, 2), ("section",) + EXPERT
    )
    in_specs = (
        P("section", EXPERT, None),
        P("section", EXPERT, None),
        P("section", None, EXPERT, None),
        P("section", None, EXPERT, None),
        P("section"),
        P("section", EXPERT, None),
        P("section", None),
        P("section", None, None),
        P("section", EXPERT, None),
        P("section", EXPERT, None, None),
        P("section", EXPERT, None, None),
        P("section", EXPERT, None, None),
    )
    out_specs = P("section", EXPERT, None)
    return jax.shard_map(shards, mesh=fine, in_specs=in_specs, out_specs=out_specs, check_vma=False)
```

```python
import functools
import math

import jax
import jax.numpy as jnp
from jax import lax
from jax.experimental import pallas as pl
from jax.experimental.pallas import tpu as pltpu
from jax.sharding import Mesh
from jax.sharding import PartitionSpec as P

EXPERTS = 128
HEAD_SIZE = 128
SPLIT = 4
CHIPS_X = 4
X = ("xh", "xl")
EXPERT = ("z", "xh", "xl", "core")
GROUP = ("z", "xh")


def shifted(shard, axis, by):
    length = lax.axis_size(axis)
    return lax.ppermute(shard, axis, [(i, (i + by) % length) for i in range(length)])


def swapped(shard, axis):
    return lax.ppermute(shard, axis, [(0, 1), (1, 0)])


def in_order(index, own, other, axis):
    return jnp.where(
        index == 0,
        jnp.concatenate([own, other], axis=axis),
        jnp.concatenate([other, own], axis=axis),
    )


def pick(array, index, axis=0):
    return lax.dynamic_index_in_dim(array, index, axis, keepdims=False)


def attention_kernel(planes, columns, block, info_ref, *refs):
    query_blocks = refs[:columns]
    key_blocks = refs[columns]
    value_blocks = refs[columns + 1 : 2 * columns + 1]
    keep_ref, send_ref, query_ref, keys, values, top, total, acc = refs[2 * columns + 1 :]
    z, x, core, fill = info_ref[0], info_ref[1], info_ref[2], info_ref[3]
    local = key_blocks.shape[3]
    fresh = (2 * local) // 3
    cached = local - fresh
    cache_rows = 2 * planes * columns * cached
    heads = query_ref.shape[0]
    half = HEAD_SIZE // 2
    first = z * (2 * columns * fresh)
    for r in range(columns):
        from_x = lax.rem(x - r + columns, columns)
        for n in range(2):
            from_core = core if n == 0 else 1 - core
            at = pl.multiple_of((from_x * 2 + from_core) * fresh, fresh)
            for head in range(heads):
                query_ref[head, pl.ds(at, fresh), :] = query_blocks[r][
                    n * fresh : (n + 1) * fresh, head * HEAD_SIZE : (head + 1) * HEAD_SIZE
                ]
    for k in range(planes):
        for r in range(columns):
            column = lax.rem(x - r + columns, columns)
            for n in range(2):
                pair = column * 2 + (core if n == 0 else 1 - core)
                for held, part, plane in (
                    (keys, key_blocks.at[k, r, n], k),
                    (values, value_blocks[r].at[k, n], lax.rem(z - k + planes, planes)),
                ):
                    device = plane * (2 * columns) + pair
                    at_cache = pl.multiple_of(device * cached, cached)
                    at_fresh = pl.multiple_of(cache_rows + device * fresh, fresh)
                    held[pl.ds(at_cache, cached), :] = part[:cached, :]
                    held[pl.ds(at_fresh, fresh), :] = part[cached:, :]
    rate = math.log2(math.e) / math.sqrt(HEAD_SIZE)

    def visit(pair, start, visible):
        for u in range(2):
            scores = lax.dot_general(
                query_ref[2 * pair + u],
                keys[pl.ds(start, block), :],
                (((1,), (1,)), ((), ())),
                preferred_element_type=jnp.float32,
            )
            if visible is not None:
                mask = visible(scores.shape)
                scores = jnp.where(mask, scores, -1e30)
            before = top[u]
            high = jnp.maximum(before, jnp.max(scores, axis=1, keepdims=True))
            weights = jnp.exp2((scores - high) * rate)
            if visible is not None:
                weights = jnp.where(mask, weights, 0.0)
            factor = jnp.exp2((before - high) * rate)
            part = weights[:, :128]
            for n in range(1, block // 128):
                part = part + weights[:, n * 128 : (n + 1) * 128]
            total[u] = total[u] * factor + part
            top[u] = high
            acc[u] = acc[u] * factor + jnp.dot(
                weights.astype(jnp.bfloat16),
                values[pl.ds(start, block), :],
                preferred_element_type=jnp.float32,
            )

    def one_pair(pair, unused):
        top[...] = jnp.full_like(top, -1e30)
        total[...] = jnp.zeros_like(total)
        acc[...] = jnp.zeros_like(acc)

        def plain(base):
            def body(n, unused):
                visit(pair, pl.multiple_of(base + n * block, block), None)
                return unused

            return body

        full = fill // block
        lax.fori_loop(0, full, plain(0), 0)

        @pl.when(fill > full * block)
        def _():
            start = pl.multiple_of(full * block, block)
            visit(
                pair,
                start,
                lambda shape: start + lax.broadcasted_iota(jnp.int32, shape, 1) < fill,
            )

        done = first // block
        lax.fori_loop(0, done, plain(cache_rows), 0)
        ahead = done * block - first
        visit(
            pair,
            pl.multiple_of(cache_rows + done * block, block),
            lambda shape: ahead + lax.broadcasted_iota(jnp.int32, shape, 1)
            <= lax.broadcasted_iota(jnp.int32, shape, 0),
        )
        heads = [acc[u] / jnp.sum(total[u], axis=1, keepdims=True) for u in range(2)]
        at = pl.multiple_of(pair * 2 * half, 2 * half)
        low = jnp.concatenate([head[:, :half] for head in heads], axis=1)
        high = jnp.concatenate([head[:, half:] for head in heads], axis=1)
        keep_ref[:, pl.ds(at, 2 * half)] = jnp.where(core == 0, low, high).astype(keep_ref.dtype)
        send_ref[:, pl.ds(at, 2 * half)] = jnp.where(core == 0, high, low).astype(send_ref.dtype)
        return unused

    lax.fori_loop(0, heads // 2, one_pair, 0)


def attend(info, query_blocks, key_blocks, value_blocks, block):
    planes, columns = key_blocks.shape[0], len(value_blocks)
    chip_rows, features = query_blocks[0].shape
    rows, heads = columns * chip_rows, features // HEAD_SIZE
    total_rows = planes * columns * 2 * key_blocks.shape[3]
    out = jax.ShapeDtypeStruct((rows, features // 2), jnp.bfloat16)
    return pl.pallas_call(
        functools.partial(attention_kernel, planes, columns, block),
        out_shape=(out, out),
        in_specs=[pl.BlockSpec(memory_space=pltpu.SMEM)]
        + [pl.BlockSpec()] * (2 * columns + 1),
        out_specs=(pl.BlockSpec(), pl.BlockSpec()),
        scratch_shapes=[
            pltpu.VMEM((heads, rows, HEAD_SIZE), jnp.bfloat16),
            pltpu.VMEM((total_rows, HEAD_SIZE), jnp.bfloat16),
            pltpu.VMEM((total_rows, HEAD_SIZE), jnp.bfloat16),
            pltpu.VMEM((2, rows, 1), jnp.float32),
            pltpu.VMEM((2, rows, 128), jnp.float32),
            pltpu.VMEM((2, rows, HEAD_SIZE), jnp.float32),
        ],
        compiler_params=pltpu.CompilerParams(vmem_limit_bytes=60 * 2**20),
    )(info, *query_blocks, key_blocks, *value_blocks)


def expert_kernel(steps, own_ref, other_ref, gate_ref, up_ref, down_ref, *refs):
    keep_ref, send_ref, gated, lifted, activation = refs
    step = pl.program_id(0)
    count = own_ref.shape[0]

    @pl.when(step == 0)
    def _():
        gated[...] = jnp.zeros_like(gated)
        lifted[...] = jnp.zeros_like(lifted)

    @pl.when(step < steps)
    def _():
        both = jnp.concatenate([own_ref[...], other_ref[...]], axis=0)
        gated[...] += jnp.dot(both, gate_ref[...], preferred_element_type=jnp.float32)
        lifted[...] += jnp.dot(both, up_ref[...], preferred_element_type=jnp.float32)

    @pl.when(step == steps - 1)
    def _():
        activation[...] = (jax.nn.silu(gated[...]) * lifted[...]).astype(activation.dtype)

    @pl.when(step >= steps)
    def _():
        output = jnp.dot(activation[...], down_ref[...], preferred_element_type=jnp.float32)
        keep_ref[...] = output[:count].astype(keep_ref.dtype)
        send_ref[...] = output[count:].astype(send_ref.dtype)


def expert(own, other, gate, up, down):
    count, width = own.shape
    hidden_units = gate.shape[1]
    steps = 4
    part = width // steps
    row_spec = pl.BlockSpec((count, part), lambda i: (0, jnp.minimum(i, steps - 1)))
    weight_spec = pl.BlockSpec((part, hidden_units), lambda i: (jnp.minimum(i, steps - 1), 0))
    tail = lambda i: (0, jnp.maximum(i - steps, 0))
    out = jax.ShapeDtypeStruct((count, width), jnp.bfloat16)
    return pl.pallas_call(
        functools.partial(expert_kernel, steps),
        grid=(2 * steps,),
        out_shape=(out, out),
        in_specs=[row_spec, row_spec, weight_spec, weight_spec]
        + [pl.BlockSpec((hidden_units, part), tail)],
        out_specs=(pl.BlockSpec((count, part), tail), pl.BlockSpec((count, part), tail)),
        scratch_shapes=[
            pltpu.VMEM((2 * count, hidden_units), jnp.float32),
            pltpu.VMEM((2 * count, hidden_units), jnp.float32),
            pltpu.VMEM((2 * count, hidden_units), jnp.bfloat16),
        ],
        compiler_params=pltpu.CompilerParams(vmem_limit_bytes=60 * 2**20),
        cost_estimate=pl.CostEstimate(
            flops=12 * count * width * hidden_units,
            bytes_accessed=6 * width * hidden_units + 8 * count * width,
            transcendentals=2 * count * hidden_units,
        ),
    )(own, other, gate, up, down)


def x_spread(block):
    return [block] + [shifted(block, X, r) for r in range(1, CHIPS_X)]


def shards(
    hidden,
    queries,
    fresh_kv,
    cache_kv,
    cache_fill,
    out_proj,
    norm_gain,
    router_weight,
    expert_labels,
    gate_proj,
    up_proj,
    down_proj,
):
    planes = lax.axis_size("z")
    z, x = lax.axis_index("z"), lax.axis_index(X)
    core = lax.axis_index("core")
    tokens, width = hidden.shape[1:]
    heads_each = planes // 2
    middle = width // 2
    kv_heads = fresh_kv.shape[3] // HEAD_SIZE

    columns = [(x + r) % CHIPS_X for r in range(CHIPS_X)]
    joined = jnp.concatenate([cache_kv[0], fresh_kv[0]], axis=1)
    joined = jnp.moveaxis(
        joined.reshape(2, joined.shape[1], kv_heads, HEAD_SIZE), 2, 0
    )
    own_kv, own_queries = pick(joined, core), pick(queries[0].reshape(tokens, 2, -1), core, 1)
    other_kv = swapped(pick(joined, 1 - core), "core")
    other_queries = swapped(pick(queries[0].reshape(tokens, 2, -1), 1 - core, 1), "core")
    chip_kv = jnp.stack([own_kv, other_kv], axis=1)
    chip_queries = jnp.concatenate([own_queries, other_queries], axis=0).reshape(
        2 * tokens, heads_each, CHIPS_X, HEAD_SIZE
    )
    key_column = jnp.stack(x_spread(chip_kv[0]))
    value_planes = [chip_kv[1]] + [shifted(chip_kv[1], "z", k) for k in range(1, planes)]
    key_blocks = lax.all_gather(key_column, "z")
    key_column, value_planes, own_rows = lax.optimization_barrier(
        (key_column, value_planes, out_proj[0])
    )
    value_blocks = x_spread(jnp.stack(value_planes))
    query_blocks = [pick(chip_queries, x, 2).reshape(2 * tokens, -1)] + [
        shifted(pick(chip_queries, columns[r], 2).reshape(2 * tokens, -1), X, r)
        for r in range(1, CHIPS_X)
    ]
    weight_rows = lax.all_gather(own_rows, "z", axis=0, tiled=True)
    info = jnp.stack([z, x, core, cache_fill[0]]).astype(jnp.int32)
    block = min(1024, planes * 8 * (joined.shape[2] - tokens))
    keep, send = attend(info, query_blocks, key_blocks, value_blocks, block)
    features = in_order(core, keep, swapped(send, "core"), 1)
    features = features.reshape(CHIPS_X, 2 * tokens, features.shape[1])

    def projection(step):
        both = jnp.dot(
            pick(features, (x + step) % CHIPS_X), weight_rows, preferred_element_type=jnp.float32
        ).reshape(2, tokens, width)
        return pick(both, core) + swapped(
            pick(both, 1 - core).astype(jnp.bfloat16), "core"
        ).astype(jnp.float32)

    def sent(part, by):
        return shifted(part.astype(jnp.bfloat16), X, by).astype(jnp.float32)

    opposite = projection(2)
    relay_up, relay_down = sent(opposite[:, :middle], 1), sent(opposite[:, middle:], -1)
    above, below = projection(1), projection(3)
    low = sent(below[:, :middle], -1) + sent(above[:, :middle] + relay_up, 1)
    high = sent(above[:, middle:], 1) + sent(below[:, middle:] + relay_down, -1)
    mixed = (
        hidden[0].astype(jnp.float32) + projection(0) + jnp.concatenate([low, high], axis=1)
    )
    inverse = lax.rsqrt(jnp.mean(mixed * mixed, axis=1, keepdims=True) + 1e-06)
    normed = (mixed * inverse * norm_gain[0].astype(jnp.float32)[None, :]).astype(jnp.bfloat16)

    label_rows = expert_labels[0]
    experts = planes * 2
    airborne = label_rows < experts
    chosen = jnp.sum(jnp.where(airborne, label_rows, 0), axis=1)
    capacity = 8
    member = (chosen[:, None] == jnp.arange(experts, dtype=jnp.int32)[None, :]).astype(jnp.int32)
    earlier = jnp.cumsum(member, axis=0) - member
    code = chosen * capacity + jnp.sum(earlier * member, axis=1)
    table = (
        code[None, :] == jnp.arange(experts * capacity, dtype=jnp.int32)[:, None]
    ).astype(jnp.bfloat16)
    packed = jnp.dot(table, normed, preferred_element_type=jnp.float32).astype(jnp.bfloat16)

    logits = jnp.dot(normed, router_weight[0], preferred_element_type=jnp.float32)
    matches = label_rows[:, :, None] == jnp.arange(EXPERTS, dtype=jnp.int32)[None, None, :]
    picked = jnp.sum(jnp.where(matches, logits[:, None, :], 0.0), axis=2)
    probabilities = jax.nn.softmax(picked, axis=1)
    combine = jnp.sum(jnp.where(airborne, probabilities, 0.0), axis=1)

    weights = (gate_proj[0, 0], up_proj[0, 0], down_proj[0, 0])
    near = lax.all_to_all(packed, GROUP, split_axis=0, concat_axis=0, tiled=True)
    near_other = swapped(near, "core")
    far = swapped(near, "xl")
    near_keep, near_send = expert(near, near_other, *weights)
    far, near_keep, near_send = lax.optimization_barrier((far, near_keep, near_send))
    far_keep, far_send = expert(far, swapped(far, "core"), *weights)

    def wide(array):
        return array.astype(jnp.float32)

    far_sum = (wide(far_keep) + wide(swapped(far_send, "core"))).astype(jnp.bfloat16)
    near_sum = wide(near_keep) + wide(swapped(near_send, "core"))
    summed = (near_sum + wide(swapped(far_sum, "xl"))).astype(jnp.bfloat16)
    returned = lax.all_to_all(summed, GROUP, split_axis=0, concat_axis=0, tiled=True)
    routed = lax.dot_general(
        table, returned, (((0,), (0,)), ((), ())), preferred_element_type=jnp.float32
    )
    result = (mixed + combine[:, None] * routed).astype(jnp.bfloat16)
    return shifted(result[None], "section", 1)


def solution(mesh):
    sections, devices = mesh.devices.shape
    planes = devices // (2 * CHIPS_X)
    fine = Mesh(
        mesh.devices.reshape(sections, planes, 2, 2, 2), ("section",) + EXPERT
    )
    in_specs = (
        P("section", EXPERT, None),
        P("section", EXPERT, None),
        P("section", None, EXPERT, None),
        P("section", None, EXPERT, None),
        P("section"),
        P("section", EXPERT, None),
        P("section", None),
        P("section", None, None),
        P("section", EXPERT, None),
        P("section", EXPERT, None, None),
        P("section", EXPERT, None, None),
        P("section", EXPERT, None, None),
    )
    out_specs = P("section", EXPERT, None)
    return jax.shard_map(shards, mesh=fine, in_specs=in_specs, out_specs=out_specs, check_vma=False)
```

```python
import functools
import math

import jax
import jax.numpy as jnp
from jax import lax
from jax.experimental import pallas as pl
from jax.experimental.pallas import tpu as pltpu
from jax.sharding import Mesh
from jax.sharding import PartitionSpec as P

EXPERTS = 128
HEAD_SIZE = 128
SPLIT = 4
CHIPS_X = 4
X = ("xh", "xl")
EXPERT = ("z", "xh", "xl", "core")
GROUP = ("z", "xh")


def shifted(shard, axis, by):
    length = lax.axis_size(axis)
    return lax.ppermute(shard, axis, [(i, (i + by) % length) for i in range(length)])


def swapped(shard, axis):
    return lax.ppermute(shard, axis, [(0, 1), (1, 0)])


def in_order(index, own, other, axis):
    return jnp.where(
        index == 0,
        jnp.concatenate([own, other], axis=axis),
        jnp.concatenate([other, own], axis=axis),
    )


def pick(array, index, axis=0):
    return lax.dynamic_index_in_dim(array, index, axis, keepdims=False)


def attention_kernel(planes, columns, block, info_ref, *refs):
    query_blocks = refs[:columns]
    key_blocks = refs[columns : columns + planes]
    value_blocks = refs[columns + planes : 2 * columns + planes]
    keep_ref, send_ref, query_ref, keys, values, top, total, acc = refs[2 * columns + planes :]
    z, x, core, fill = info_ref[0], info_ref[1], info_ref[2], info_ref[3]
    local = key_blocks[0].shape[2]
    fresh = (2 * local) // 3
    cached = local - fresh
    cache_rows = 2 * planes * columns * cached
    heads = query_ref.shape[0]
    half = HEAD_SIZE // 2
    first = z * (2 * columns * fresh)
    for r in range(columns):
        from_x = lax.rem(x - r + columns, columns)
        for n in range(2):
            from_core = core if n == 0 else 1 - core
            at = pl.multiple_of((from_x * 2 + from_core) * fresh, fresh)
            for head in range(heads):
                query_ref[head, pl.ds(at, fresh), :] = query_blocks[r][
                    n * fresh : (n + 1) * fresh, head * HEAD_SIZE : (head + 1) * HEAD_SIZE
                ]
    for k in range(planes):
        plane = lax.rem(z - k + planes, planes)
        for r in range(columns):
            chip = plane * columns + lax.rem(x - r + columns, columns)
            for n in range(2):
                device = chip * 2 + (core if n == 0 else 1 - core)
                at_cache = pl.multiple_of(device * cached, cached)
                at_fresh = pl.multiple_of(cache_rows + device * fresh, fresh)
                for held, part in ((keys, key_blocks[k]), (values, value_blocks[r])):
                    where = (r, n) if held is keys else (k, n)
                    held[pl.ds(at_cache, cached), :] = part[where[0], where[1], :cached, :]
                    held[pl.ds(at_fresh, fresh), :] = part[where[0], where[1], cached:, :]
    rate = math.log2(math.e) / math.sqrt(HEAD_SIZE)

    def score(head, start):
        return lax.dot_general(
            query_ref[head],
            keys[pl.ds(start, block), :],
            (((1,), (1,)), ((), ())),
            preferred_element_type=jnp.float32,
        )

    def visit(start, visible):
        ahead = score(0, start)
        for head in range(heads):
            scores = ahead
            if head + 1 < heads:
                ahead = score(head + 1, start)
            if visible is not None:
                mask = visible(scores.shape)
                scores = jnp.where(mask, scores, -1e30)
            before = top[head]
            high = jnp.maximum(before, jnp.max(scores, axis=1, keepdims=True))
            weights = jnp.exp2((scores - high) * rate)
            if visible is not None:
                weights = jnp.where(mask, weights, 0.0)
            factor = jnp.exp2((before - high) * rate)
            part = weights[:, :128]
            for n in range(1, block // 128):
                part = part + weights[:, n * 128 : (n + 1) * 128]
            total[head] = total[head] * factor + part
            top[head] = high
            acc[head] = acc[head] * factor + jnp.dot(
                weights.astype(jnp.bfloat16),
                values[pl.ds(start, block), :],
                preferred_element_type=jnp.float32,
            )

    top[...] = jnp.full_like(top, -1e30)
    total[...] = jnp.zeros_like(total)
    acc[...] = jnp.zeros_like(acc)

    def plain(base):
        def body(n, unused):
            visit(pl.multiple_of(base + n * block, block), None)
            return unused

        return body

    full = fill // block
    lax.fori_loop(0, full, plain(0), 0)

    @pl.when(fill > full * block)
    def _():
        start = pl.multiple_of(full * block, block)
        visit(start, lambda shape: start + lax.broadcasted_iota(jnp.int32, shape, 1) < fill)

    done = first // block
    lax.fori_loop(0, done, plain(cache_rows), 0)
    offset = done * block - first
    visit(
        pl.multiple_of(cache_rows + done * block, block),
        lambda shape: offset + lax.broadcasted_iota(jnp.int32, shape, 1)
        <= lax.broadcasted_iota(jnp.int32, shape, 0),
    )
    for pair in range(heads // 2):
        both = [
            acc[2 * pair + u] / jnp.sum(total[2 * pair + u], axis=1, keepdims=True)
            for u in range(2)
        ]
        low = jnp.concatenate([head[:, :half] for head in both], axis=1)
        high = jnp.concatenate([head[:, half:] for head in both], axis=1)
        at = slice(pair * 2 * half, (pair + 1) * 2 * half)
        keep_ref[:, at] = jnp.where(core == 0, low, high).astype(keep_ref.dtype)
        send_ref[:, at] = jnp.where(core == 0, high, low).astype(send_ref.dtype)


def attend(info, query_blocks, key_blocks, value_blocks, block):
    planes, columns = len(key_blocks), len(value_blocks)
    chip_rows, features = query_blocks[0].shape
    rows, heads = columns * chip_rows, features // HEAD_SIZE
    total_rows = planes * columns * 2 * key_blocks[0].shape[2]
    out = jax.ShapeDtypeStruct((rows, features // 2), jnp.bfloat16)
    return pl.pallas_call(
        functools.partial(attention_kernel, planes, columns, block),
        out_shape=(out, out),
        in_specs=[pl.BlockSpec(memory_space=pltpu.SMEM)]
        + [pl.BlockSpec()] * (2 * columns + planes),
        out_specs=(pl.BlockSpec(), pl.BlockSpec()),
        scratch_shapes=[
            pltpu.VMEM((heads, rows, HEAD_SIZE), jnp.bfloat16),
            pltpu.VMEM((total_rows, HEAD_SIZE), jnp.bfloat16),
            pltpu.VMEM((total_rows, HEAD_SIZE), jnp.bfloat16),
            pltpu.VMEM((heads, rows, 1), jnp.float32),
            pltpu.VMEM((heads, rows, 128), jnp.float32),
            pltpu.VMEM((heads, rows, HEAD_SIZE), jnp.float32),
        ],
        compiler_params=pltpu.CompilerParams(vmem_limit_bytes=60 * 2**20),
    )(info, *query_blocks, *key_blocks, *value_blocks)


def expert_kernel(steps, own_ref, other_ref, gate_ref, up_ref, down_ref, *refs):
    keep_ref, send_ref, gated, lifted, activation = refs
    step = pl.program_id(0)
    count = own_ref.shape[0]

    @pl.when(step == 0)
    def _():
        gated[...] = jnp.zeros_like(gated)
        lifted[...] = jnp.zeros_like(lifted)

    @pl.when(step < steps)
    def _():
        both = jnp.concatenate([own_ref[...], other_ref[...]], axis=0)
        gated[...] += jnp.dot(both, gate_ref[...], preferred_element_type=jnp.float32)
        lifted[...] += jnp.dot(both, up_ref[...], preferred_element_type=jnp.float32)

    @pl.when(step == steps - 1)
    def _():
        activation[...] = (jax.nn.silu(gated[...]) * lifted[...]).astype(activation.dtype)

    @pl.when(step >= steps)
    def _():
        output = jnp.dot(activation[...], down_ref[...], preferred_element_type=jnp.float32)
        keep_ref[...] = output[:count].astype(keep_ref.dtype)
        send_ref[...] = output[count:].astype(send_ref.dtype)


def expert(own, other, gate, up, down):
    count, width = own.shape
    hidden_units = gate.shape[1]
    steps = 4
    part = width // steps
    row_spec = pl.BlockSpec((count, part), lambda i: (0, jnp.minimum(i, steps - 1)))
    weight_spec = pl.BlockSpec((part, hidden_units), lambda i: (jnp.minimum(i, steps - 1), 0))
    tail = lambda i: (0, jnp.maximum(i - steps, 0))
    out = jax.ShapeDtypeStruct((count, width), jnp.bfloat16)
    return pl.pallas_call(
        functools.partial(expert_kernel, steps),
        grid=(2 * steps,),
        out_shape=(out, out),
        in_specs=[row_spec, row_spec, weight_spec, weight_spec]
        + [pl.BlockSpec((hidden_units, part), tail)],
        out_specs=(pl.BlockSpec((count, part), tail), pl.BlockSpec((count, part), tail)),
        scratch_shapes=[
            pltpu.VMEM((2 * count, hidden_units), jnp.float32),
            pltpu.VMEM((2 * count, hidden_units), jnp.float32),
            pltpu.VMEM((2 * count, hidden_units), jnp.bfloat16),
        ],
        compiler_params=pltpu.CompilerParams(vmem_limit_bytes=20 * 2**20),
        cost_estimate=pl.CostEstimate(
            flops=12 * count * width * hidden_units,
            bytes_accessed=6 * width * hidden_units + 8 * count * width,
            transcendentals=2 * count * hidden_units,
        ),
    )(own, other, gate, up, down)


def x_spread(block):
    return [block] + [shifted(block, X, r) for r in range(1, CHIPS_X)]


def shards(
    hidden,
    queries,
    fresh_kv,
    cache_kv,
    cache_fill,
    out_proj,
    norm_gain,
    router_weight,
    expert_labels,
    gate_proj,
    up_proj,
    down_proj,
):
    planes = lax.axis_size("z")
    z, x = lax.axis_index("z"), lax.axis_index(X)
    core = lax.axis_index("core")
    tokens, width = hidden.shape[1:]
    heads_each = planes // 2
    middle = width // 2
    kv_heads = fresh_kv.shape[3] // HEAD_SIZE

    columns = [(x + r) % CHIPS_X for r in range(CHIPS_X)]
    joined = jnp.concatenate([cache_kv[0], fresh_kv[0]], axis=1)
    joined = jnp.moveaxis(
        joined.reshape(2, joined.shape[1], kv_heads, HEAD_SIZE), 2, 0
    )
    own_kv, own_queries = pick(joined, core), pick(queries[0].reshape(tokens, 2, -1), core, 1)
    other_kv = swapped(pick(joined, 1 - core), "core")
    other_queries = swapped(pick(queries[0].reshape(tokens, 2, -1), 1 - core, 1), "core")
    chip_kv = jnp.stack([own_kv, other_kv], axis=1)
    chip_queries = jnp.concatenate([own_queries, other_queries], axis=0).reshape(
        2 * tokens, heads_each, CHIPS_X, HEAD_SIZE
    )
    key_column = jnp.stack(x_spread(chip_kv[0]))
    query_blocks = [pick(chip_queries, x, 2).reshape(2 * tokens, -1)] + [
        shifted(pick(chip_queries, columns[r], 2).reshape(2 * tokens, -1), X, r)
        for r in range(1, CHIPS_X)
    ]
    value_planes = [chip_kv[1]] + [shifted(chip_kv[1], "z", k) for k in range(1, planes)]
    key_column, value_planes, query_blocks = lax.optimization_barrier(
        (key_column, value_planes, query_blocks)
    )
    value_blocks = x_spread(jnp.stack(value_planes))
    key_blocks = [key_column] * planes
    for k in range(1, planes // 2 + 1):
        key_blocks[k] = shifted(key_blocks[k - 1], "z", 1)
        if k < planes - k:
            key_blocks[planes - k] = shifted(key_blocks[(planes - k + 1) % planes], "z", -1)
    weight_rows = lax.all_gather(out_proj[0], "z", axis=0, tiled=True)
    info = jnp.stack([z, x, core, cache_fill[0]]).astype(jnp.int32)
    block = min(1024, planes * 8 * (joined.shape[2] - tokens))
    keep, send = attend(info, query_blocks, key_blocks, value_blocks, block)
    features = in_order(core, keep, swapped(send, "core"), 1)
    features = features.reshape(CHIPS_X, 2 * tokens, features.shape[1])

    def projection(step):
        both = jnp.dot(
            pick(features, (x + step) % CHIPS_X), weight_rows, preferred_element_type=jnp.float32
        ).reshape(2, tokens, width)
        return pick(both, core) + swapped(
            pick(both, 1 - core).astype(jnp.bfloat16), "core"
        ).astype(jnp.float32)

    def sent(part, by):
        return shifted(part.astype(jnp.bfloat16), X, by).astype(jnp.float32)

    opposite = projection(2)
    relay_up, relay_down = sent(opposite[:, :middle], 1), sent(opposite[:, middle:], -1)
    above, below = projection(1), projection(3)
    low = sent(below[:, :middle], -1) + sent(above[:, :middle] + relay_up, 1)
    high = sent(above[:, middle:], 1) + sent(below[:, middle:] + relay_down, -1)
    mixed = (
        hidden[0].astype(jnp.float32) + projection(0) + jnp.concatenate([low, high], axis=1)
    )
    inverse = lax.rsqrt(jnp.mean(mixed * mixed, axis=1, keepdims=True) + 1e-06)
    normed = (mixed * inverse * norm_gain[0].astype(jnp.float32)[None, :]).astype(jnp.bfloat16)

    label_rows = expert_labels[0]
    experts = planes * 2
    airborne = label_rows < experts
    chosen = jnp.sum(jnp.where(airborne, label_rows, 0), axis=1)
    capacity = 8
    member = (chosen[:, None] == jnp.arange(experts, dtype=jnp.int32)[None, :]).astype(jnp.int32)
    earlier = jnp.cumsum(member, axis=0) - member
    code = chosen * capacity + jnp.sum(earlier * member, axis=1)
    table = (
        code[None, :] == jnp.arange(experts * capacity, dtype=jnp.int32)[:, None]
    ).astype(jnp.bfloat16)
    packed = jnp.dot(table, normed, preferred_element_type=jnp.float32).astype(jnp.bfloat16)

    logits = jnp.dot(normed, router_weight[0], preferred_element_type=jnp.float32)
    matches = label_rows[:, :, None] == jnp.arange(EXPERTS, dtype=jnp.int32)[None, None, :]
    picked = jnp.sum(jnp.where(matches, logits[:, None, :], 0.0), axis=2)
    probabilities = jax.nn.softmax(picked, axis=1)
    combine = jnp.sum(jnp.where(airborne, probabilities, 0.0), axis=1)

    weights = (gate_proj[0, 0], up_proj[0, 0], down_proj[0, 0])
    near = lax.all_to_all(packed, GROUP, split_axis=0, concat_axis=0, tiled=True)
    near_other = swapped(near, "core")
    far = swapped(near, "xl")
    near_keep, near_send = expert(near, near_other, *weights)
    far, near_keep, near_send = lax.optimization_barrier((far, near_keep, near_send))
    far_keep, far_send = expert(far, swapped(far, "core"), *weights)

    def wide(array):
        return array.astype(jnp.float32)

    far_sum = (wide(far_keep) + wide(swapped(far_send, "core"))).astype(jnp.bfloat16)
    near_sum = wide(near_keep) + wide(swapped(near_send, "core"))
    summed = (near_sum + wide(swapped(far_sum, "xl"))).astype(jnp.bfloat16)
    returned = lax.all_to_all(summed, GROUP, split_axis=0, concat_axis=0, tiled=True)
    routed = lax.dot_general(
        table, returned, (((0,), (0,)), ((), ())), preferred_element_type=jnp.float32
    )
    result = (mixed + combine[:, None] * routed).astype(jnp.bfloat16)
    return shifted(result[None], "section", 1)


def solution(mesh):
    sections, devices = mesh.devices.shape
    planes = devices // (2 * CHIPS_X)
    fine = Mesh(
        mesh.devices.reshape(sections, planes, 2, 2, 2), ("section",) + EXPERT
    )
    in_specs = (
        P("section", EXPERT, None),
        P("section", EXPERT, None),
        P("section", None, EXPERT, None),
        P("section", None, EXPERT, None),
        P("section"),
        P("section", EXPERT, None),
        P("section", None),
        P("section", None, None),
        P("section", EXPERT, None),
        P("section", EXPERT, None, None),
        P("section", EXPERT, None, None),
        P("section", EXPERT, None, None),
    )
    out_specs = P("section", EXPERT, None)
    return jax.shard_map(shards, mesh=fine, in_specs=in_specs, out_specs=out_specs, check_vma=False)
```

```python
import functools
import math

import jax
import jax.numpy as jnp
from jax import lax
from jax.experimental import pallas as pl
from jax.experimental.pallas import tpu as pltpu
from jax.sharding import Mesh
from jax.sharding import PartitionSpec as P

EXPERTS = 128
HEAD_SIZE = 128
SPLIT = 4
CHIPS_X = 4
X = ("xh", "xl")
EXPERT = ("z", "xh", "xl", "core")
GROUP = ("z", "xh")


def shifted(shard, axis, by):
    length = lax.axis_size(axis)
    return lax.ppermute(shard, axis, [(i, (i + by) % length) for i in range(length)])


def swapped(shard, axis):
    return lax.ppermute(shard, axis, [(0, 1), (1, 0)])


def in_order(index, own, other, axis):
    return jnp.where(
        index == 0,
        jnp.concatenate([own, other], axis=axis),
        jnp.concatenate([other, own], axis=axis),
    )


def pick(array, index, axis=0):
    return lax.dynamic_index_in_dim(array, index, axis, keepdims=False)


def attention_kernel(planes, columns, block, info_ref, *refs):
    query_blocks = refs[:columns]
    key_blocks = refs[columns : columns + planes]
    value_blocks = refs[columns + planes : 2 * columns + planes]
    keep_ref, send_ref, query_ref, keys, values, top, total, acc = refs[2 * columns + planes :]
    z, x, core, fill = info_ref[0], info_ref[1], info_ref[2], info_ref[3]
    local = key_blocks[0].shape[2]
    fresh = (2 * local) // 3
    cached = local - fresh
    cache_rows = 2 * planes * columns * cached
    heads = query_ref.shape[0]
    half = HEAD_SIZE // 2
    first = z * (2 * columns * fresh)
    for r in range(columns):
        from_x = lax.rem(x - r + columns, columns)
        for n in range(2):
            from_core = core if n == 0 else 1 - core
            at = pl.multiple_of((from_x * 2 + from_core) * fresh, fresh)
            for head in range(heads):
                query_ref[head, pl.ds(at, fresh), :] = query_blocks[r][
                    n * fresh : (n + 1) * fresh, head * HEAD_SIZE : (head + 1) * HEAD_SIZE
                ]
    for k in range(planes):
        plane = lax.rem(z - k + planes, planes)
        for r in range(columns):
            chip = plane * columns + lax.rem(x - r + columns, columns)
            for n in range(2):
                device = chip * 2 + (core if n == 0 else 1 - core)
                at_cache = pl.multiple_of(device * cached, cached)
                at_fresh = pl.multiple_of(cache_rows + device * fresh, fresh)
                for held, part in ((keys, key_blocks[k]), (values, value_blocks[r])):
                    where = (r, n) if held is keys else (k, n)
                    held[pl.ds(at_cache, cached), :] = part[where[0], where[1], :cached, :]
                    held[pl.ds(at_fresh, fresh), :] = part[where[0], where[1], cached:, :]
    rate = math.log2(math.e) / math.sqrt(HEAD_SIZE)

    def score(head, start):
        return lax.dot_general(
            query_ref[head],
            keys[pl.ds(start, block), :],
            (((1,), (1,)), ((), ())),
            preferred_element_type=jnp.float32,
        )

    def visit(start, visible):
        ahead = score(0, start)
        for head in range(heads):
            scores = ahead
            if head + 1 < heads:
                ahead = score(head + 1, start)
            if visible is not None:
                mask = visible(scores.shape)
                scores = jnp.where(mask, scores, -1e30)
            before = top[head]
            high = jnp.maximum(before, jnp.max(scores, axis=1, keepdims=True))
            weights = jnp.exp2((scores - high) * rate)
            if visible is not None:
                weights = jnp.where(mask, weights, 0.0)
            factor = jnp.exp2((before - high) * rate)
            part = weights[:, :128]
            for n in range(1, block // 128):
                part = part + weights[:, n * 128 : (n + 1) * 128]
            total[head] = total[head] * factor + part
            top[head] = high
            acc[head] = acc[head] * factor + jnp.dot(
                weights.astype(jnp.bfloat16),
                values[pl.ds(start, block), :],
                preferred_element_type=jnp.float32,
            )

    top[...] = jnp.full_like(top, -1e30)
    total[...] = jnp.zeros_like(total)
    acc[...] = jnp.zeros_like(acc)

    def plain(base):
        def body(n, unused):
            visit(pl.multiple_of(base + n * block, block), None)
            return unused

        return body

    full = fill // block
    lax.fori_loop(0, full, plain(0), 0)

    @pl.when(fill > full * block)
    def _():
        start = pl.multiple_of(full * block, block)
        visit(start, lambda shape: start + lax.broadcasted_iota(jnp.int32, shape, 1) < fill)

    done = first // block
    lax.fori_loop(0, done, plain(cache_rows), 0)
    offset = done * block - first
    visit(
        pl.multiple_of(cache_rows + done * block, block),
        lambda shape: offset + lax.broadcasted_iota(jnp.int32, shape, 1)
        <= lax.broadcasted_iota(jnp.int32, shape, 0),
    )
    for pair in range(heads // 2):
        both = [
            acc[2 * pair + u] / jnp.sum(total[2 * pair + u], axis=1, keepdims=True)
            for u in range(2)
        ]
        low = jnp.concatenate([head[:, :half] for head in both], axis=1)
        high = jnp.concatenate([head[:, half:] for head in both], axis=1)
        at = slice(pair * 2 * half, (pair + 1) * 2 * half)
        keep_ref[:, at] = jnp.where(core == 0, low, high).astype(keep_ref.dtype)
        send_ref[:, at] = jnp.where(core == 0, high, low).astype(send_ref.dtype)


def attend(info, query_blocks, key_blocks, value_blocks, block):
    planes, columns = len(key_blocks), len(value_blocks)
    chip_rows, features = query_blocks[0].shape
    rows, heads = columns * chip_rows, features // HEAD_SIZE
    total_rows = planes * columns * 2 * key_blocks[0].shape[2]
    out = jax.ShapeDtypeStruct((rows, features // 2), jnp.bfloat16)
    return pl.pallas_call(
        functools.partial(attention_kernel, planes, columns, block),
        out_shape=(out, out),
        in_specs=[pl.BlockSpec(memory_space=pltpu.SMEM)]
        + [pl.BlockSpec()] * (2 * columns + planes),
        out_specs=(pl.BlockSpec(), pl.BlockSpec()),
        scratch_shapes=[
            pltpu.VMEM((heads, rows, HEAD_SIZE), jnp.bfloat16),
            pltpu.VMEM((total_rows, HEAD_SIZE), jnp.bfloat16),
            pltpu.VMEM((total_rows, HEAD_SIZE), jnp.bfloat16),
            pltpu.VMEM((heads, rows, 1), jnp.float32),
            pltpu.VMEM((heads, rows, 128), jnp.float32),
            pltpu.VMEM((heads, rows, HEAD_SIZE), jnp.float32),
        ],
        compiler_params=pltpu.CompilerParams(vmem_limit_bytes=60 * 2**20),
    )(info, *query_blocks, *key_blocks, *value_blocks)


def expert_kernel(steps, own_ref, other_ref, gate_ref, up_ref, down_ref, *refs):
    keep_ref, send_ref, gated, lifted, activation = refs
    step = pl.program_id(0)
    count = own_ref.shape[0]

    @pl.when(step == 0)
    def _():
        gated[...] = jnp.zeros_like(gated)
        lifted[...] = jnp.zeros_like(lifted)

    @pl.when(step < steps)
    def _():
        both = jnp.concatenate([own_ref[...], other_ref[...]], axis=0)
        gated[...] += jnp.dot(both, gate_ref[...], preferred_element_type=jnp.float32)
        lifted[...] += jnp.dot(both, up_ref[...], preferred_element_type=jnp.float32)

    @pl.when(step == steps - 1)
    def _():
        activation[...] = (jax.nn.silu(gated[...]) * lifted[...]).astype(activation.dtype)

    @pl.when(step >= steps)
    def _():
        output = jnp.dot(activation[...], down_ref[...], preferred_element_type=jnp.float32)
        keep_ref[...] = output[:count].astype(keep_ref.dtype)
        send_ref[...] = output[count:].astype(send_ref.dtype)


def expert(own, other, gate, up, down):
    count, width = own.shape
    hidden_units = gate.shape[1]
    steps = 4
    part = width // steps
    row_spec = pl.BlockSpec((count, part), lambda i: (0, jnp.minimum(i, steps - 1)))
    weight_spec = pl.BlockSpec((part, hidden_units), lambda i: (jnp.minimum(i, steps - 1), 0))
    tail = lambda i: (0, jnp.maximum(i - steps, 0))
    out = jax.ShapeDtypeStruct((count, width), jnp.bfloat16)
    return pl.pallas_call(
        functools.partial(expert_kernel, steps),
        grid=(2 * steps,),
        out_shape=(out, out),
        in_specs=[row_spec, row_spec, weight_spec, weight_spec]
        + [pl.BlockSpec((hidden_units, part), tail)],
        out_specs=(pl.BlockSpec((count, part), tail), pl.BlockSpec((count, part), tail)),
        scratch_shapes=[
            pltpu.VMEM((2 * count, hidden_units), jnp.float32),
            pltpu.VMEM((2 * count, hidden_units), jnp.float32),
            pltpu.VMEM((2 * count, hidden_units), jnp.bfloat16),
        ],
        compiler_params=pltpu.CompilerParams(vmem_limit_bytes=20 * 2**20),
        cost_estimate=pl.CostEstimate(
            flops=12 * count * width * hidden_units,
            bytes_accessed=6 * width * hidden_units + 8 * count * width,
            transcendentals=2 * count * hidden_units,
        ),
    )(own, other, gate, up, down)


def x_spread(block):
    return [block] + [shifted(block, X, r) for r in range(1, CHIPS_X)]


def shards(
    hidden,
    queries,
    fresh_kv,
    cache_kv,
    cache_fill,
    out_proj,
    norm_gain,
    router_weight,
    expert_labels,
    gate_proj,
    up_proj,
    down_proj,
):
    planes = lax.axis_size("z")
    z, x = lax.axis_index("z"), lax.axis_index(X)
    core = lax.axis_index("core")
    tokens, width = hidden.shape[1:]
    heads_each = planes // 2
    middle = width // 2
    kv_heads = fresh_kv.shape[3] // HEAD_SIZE

    columns = [(x + r) % CHIPS_X for r in range(CHIPS_X)]
    joined = jnp.concatenate([cache_kv[0], fresh_kv[0]], axis=1)
    joined = jnp.moveaxis(
        joined.reshape(2, joined.shape[1], kv_heads, HEAD_SIZE), 2, 0
    )
    own_kv, own_queries = pick(joined, core), pick(queries[0].reshape(tokens, 2, -1), core, 1)
    other_kv = swapped(pick(joined, 1 - core), "core")
    other_queries = swapped(pick(queries[0].reshape(tokens, 2, -1), 1 - core, 1), "core")
    chip_kv = jnp.stack([own_kv, other_kv], axis=1)
    chip_queries = jnp.concatenate([own_queries, other_queries], axis=0).reshape(
        2 * tokens, heads_each, CHIPS_X, HEAD_SIZE
    )
    key_column = jnp.stack(x_spread(chip_kv[0]))
    query_blocks = [pick(chip_queries, x, 2).reshape(2 * tokens, -1)] + [
        shifted(pick(chip_queries, columns[r], 2).reshape(2 * tokens, -1), X, r)
        for r in range(1, CHIPS_X)
    ]
    value_planes = [chip_kv[1]] + [shifted(chip_kv[1], "z", k) for k in range(1, planes)]
    key_blocks = [key_column] * planes
    for k in range(1, planes // 2 + 1):
        key_blocks[k] = shifted(key_blocks[k - 1], "z", 1)
        if k < planes - k:
            key_blocks[planes - k] = shifted(key_blocks[(planes - k + 1) % planes], "z", -1)
        if k == 1:
            key_blocks, value_planes = lax.optimization_barrier((key_blocks, value_planes))
            value_blocks = x_spread(jnp.stack(value_planes))
        if k == 2:
            key_blocks, query_blocks = lax.optimization_barrier((key_blocks, query_blocks))
        if k == 3:
            key_blocks, value_blocks[1] = lax.optimization_barrier((key_blocks, value_blocks[1]))
    weight_rows = lax.all_gather(out_proj[0], "z", axis=0, tiled=True)
    info = jnp.stack([z, x, core, cache_fill[0]]).astype(jnp.int32)
    block = min(1024, planes * 8 * (joined.shape[2] - tokens))
    keep, send = attend(info, query_blocks, key_blocks, value_blocks, block)
    features = in_order(core, keep, swapped(send, "core"), 1)
    features = features.reshape(CHIPS_X, 2 * tokens, features.shape[1])

    def projection(step):
        both = jnp.dot(
            pick(features, (x + step) % CHIPS_X), weight_rows, preferred_element_type=jnp.float32
        ).reshape(2, tokens, width)
        return pick(both, core) + swapped(
            pick(both, 1 - core).astype(jnp.bfloat16), "core"
        ).astype(jnp.float32)

    def sent(part, by):
        return shifted(part.astype(jnp.bfloat16), X, by).astype(jnp.float32)

    opposite = projection(2)
    relay_up, relay_down = sent(opposite[:, :middle], 1), sent(opposite[:, middle:], -1)
    above, below = projection(1), projection(3)
    low = sent(below[:, :middle], -1) + sent(above[:, :middle] + relay_up, 1)
    high = sent(above[:, middle:], 1) + sent(below[:, middle:] + relay_down, -1)
    mixed = (
        hidden[0].astype(jnp.float32) + projection(0) + jnp.concatenate([low, high], axis=1)
    )
    inverse = lax.rsqrt(jnp.mean(mixed * mixed, axis=1, keepdims=True) + 1e-06)
    normed = (mixed * inverse * norm_gain[0].astype(jnp.float32)[None, :]).astype(jnp.bfloat16)

    label_rows = expert_labels[0]
    experts = planes * 2
    airborne = label_rows < experts
    chosen = jnp.sum(jnp.where(airborne, label_rows, 0), axis=1)
    capacity = 8
    member = (chosen[:, None] == jnp.arange(experts, dtype=jnp.int32)[None, :]).astype(jnp.int32)
    earlier = jnp.cumsum(member, axis=0) - member
    code = chosen * capacity + jnp.sum(earlier * member, axis=1)
    table = (
        code[None, :] == jnp.arange(experts * capacity, dtype=jnp.int32)[:, None]
    ).astype(jnp.bfloat16)
    packed = jnp.dot(table, normed, preferred_element_type=jnp.float32).astype(jnp.bfloat16)

    logits = jnp.dot(normed, router_weight[0], preferred_element_type=jnp.float32)
    matches = label_rows[:, :, None] == jnp.arange(EXPERTS, dtype=jnp.int32)[None, None, :]
    picked = jnp.sum(jnp.where(matches, logits[:, None, :], 0.0), axis=2)
    probabilities = jax.nn.softmax(picked, axis=1)
    combine = jnp.sum(jnp.where(airborne, probabilities, 0.0), axis=1)

    weights = (gate_proj[0, 0], up_proj[0, 0], down_proj[0, 0])
    near = lax.all_to_all(packed, GROUP, split_axis=0, concat_axis=0, tiled=True)
    near_other = swapped(near, "core")
    far = swapped(near, "xl")
    near_keep, near_send = expert(near, near_other, *weights)
    far, near_keep, near_send = lax.optimization_barrier((far, near_keep, near_send))
    far_keep, far_send = expert(far, swapped(far, "core"), *weights)

    def wide(array):
        return array.astype(jnp.float32)

    far_sum = (wide(far_keep) + wide(swapped(far_send, "core"))).astype(jnp.bfloat16)
    near_sum = wide(near_keep) + wide(swapped(near_send, "core"))
    parts = (slice(0, middle), slice(middle, width))
    far_parts = [far_sum[:, part] for part in parts]
    back = [swapped(far_parts[0], "xl"), far_parts[1]]
    back = list(lax.optimization_barrier(tuple(back)))
    back[1] = swapped(back[1], "xl")
    finished = []
    for n, part in enumerate(parts):
        summed = (near_sum[:, part] + wide(back[n])).astype(jnp.bfloat16)
        returned = lax.all_to_all(summed, GROUP, split_axis=0, concat_axis=0, tiled=True)
        if not finished:
            returned, back[1] = lax.optimization_barrier((returned, back[1]))
        routed = lax.dot_general(
            table, returned, (((0,), (0,)), ((), ())), preferred_element_type=jnp.float32
        )
        result = (mixed[:, part] + combine[:, None] * routed).astype(jnp.bfloat16)
        finished.append(shifted(result, "section", 1))
    return jnp.concatenate(finished, axis=1)[None]


def solution(mesh):
    sections, devices = mesh.devices.shape
    planes = devices // (2 * CHIPS_X)
    fine = Mesh(
        mesh.devices.reshape(sections, planes, 2, 2, 2), ("section",) + EXPERT
    )
    in_specs = (
        P("section", EXPERT, None),
        P("section", EXPERT, None),
        P("section", None, EXPERT, None),
        P("section", None, EXPERT, None),
        P("section"),
        P("section", EXPERT, None),
        P("section", None),
        P("section", None, None),
        P("section", EXPERT, None),
        P("section", EXPERT, None, None),
        P("section", EXPERT, None, None),
        P("section", EXPERT, None, None),
    )
    out_specs = P("section", EXPERT, None)
    return jax.shard_map(shards, mesh=fine, in_specs=in_specs, out_specs=out_specs, check_vma=False)
```

```python
import functools
import math

import jax
import jax.numpy as jnp
from jax import lax
from jax.experimental import pallas as pl
from jax.experimental.pallas import tpu as pltpu
from jax.sharding import Mesh
from jax.sharding import PartitionSpec as P

EXPERTS = 128
HEAD_SIZE = 128
SPLIT = 4
CHIPS_X = 4
X = ("xh", "xl")
EXPERT = ("z", "xh", "xl", "core")
GROUP = ("z", "xh")


def shifted(shard, axis, by):
    length = lax.axis_size(axis)
    return lax.ppermute(shard, axis, [(i, (i + by) % length) for i in range(length)])


def swapped(shard, axis):
    return lax.ppermute(shard, axis, [(0, 1), (1, 0)])


def in_order(index, own, other, axis):
    return jnp.where(
        index == 0,
        jnp.concatenate([own, other], axis=axis),
        jnp.concatenate([other, own], axis=axis),
    )


def pick(array, index, axis=0):
    return lax.dynamic_index_in_dim(array, index, axis, keepdims=False)


def attention_kernel(planes, columns, block, info_ref, *refs):
    query_blocks = refs[:columns]
    key_blocks = refs[columns : columns + planes]
    value_blocks = refs[columns + planes : 2 * columns + planes]
    keep_ref, send_ref, query_ref, keys, values, top, total, acc = refs[2 * columns + planes :]
    z, x, core, fill = info_ref[0], info_ref[1], info_ref[2], info_ref[3]
    local = key_blocks[0].shape[2]
    fresh = (2 * local) // 3
    cached = local - fresh
    cache_rows = 2 * planes * columns * cached
    heads = query_ref.shape[0]
    half = HEAD_SIZE // 2
    first = z * (2 * columns * fresh)
    for r in range(columns):
        from_x = lax.rem(x - r + columns, columns)
        for n in range(2):
            from_core = core if n == 0 else 1 - core
            at = pl.multiple_of((from_x * 2 + from_core) * fresh, fresh)
            for head in range(heads):
                query_ref[head, pl.ds(at, fresh), :] = query_blocks[r][
                    n * fresh : (n + 1) * fresh, head * HEAD_SIZE : (head + 1) * HEAD_SIZE
                ]
    for k in range(planes):
        plane = lax.rem(z - k + planes, planes)
        for r in range(columns):
            chip = plane * columns + lax.rem(x - r + columns, columns)
            for n in range(2):
                device = chip * 2 + (core if n == 0 else 1 - core)
                at_cache = pl.multiple_of(device * cached, cached)
                at_fresh = pl.multiple_of(cache_rows + device * fresh, fresh)
                for held, part in ((keys, key_blocks[k]), (values, value_blocks[r])):
                    where = (r, n) if held is keys else (k, n)
                    held[pl.ds(at_cache, cached), :] = part[where[0], where[1], :cached, :]
                    held[pl.ds(at_fresh, fresh), :] = part[where[0], where[1], cached:, :]
    rate = math.log2(math.e) / math.sqrt(HEAD_SIZE)

    def score(head, start):
        return lax.dot_general(
            query_ref[head],
            keys[pl.ds(start, block), :],
            (((1,), (1,)), ((), ())),
            preferred_element_type=jnp.float32,
        )

    def visit(start, visible):
        ahead = score(0, start)
        for head in range(heads):
            scores = ahead
            if head + 1 < heads:
                ahead = score(head + 1, start)
            if visible is not None:
                mask = visible(scores.shape)
                scores = jnp.where(mask, scores, -1e30)
            before = top[head]
            high = jnp.maximum(before, jnp.max(scores, axis=1, keepdims=True))
            weights = jnp.exp2((scores - high) * rate)
            if visible is not None:
                weights = jnp.where(mask, weights, 0.0)
            factor = jnp.exp2((before - high) * rate)
            part = weights[:, :128]
            for n in range(1, block // 128):
                part = part + weights[:, n * 128 : (n + 1) * 128]
            total[head] = total[head] * factor + part
            top[head] = high
            acc[head] = acc[head] * factor + jnp.dot(
                weights.astype(jnp.bfloat16),
                values[pl.ds(start, block), :],
                preferred_element_type=jnp.float32,
            )

    top[...] = jnp.full_like(top, -1e30)
    total[...] = jnp.zeros_like(total)
    acc[...] = jnp.zeros_like(acc)

    def plain(base):
        def body(n, unused):
            visit(pl.multiple_of(base + n * block, block), None)
            return unused

        return body

    full = fill // block
    lax.fori_loop(0, full, plain(0), 0)

    @pl.when(fill > full * block)
    def _():
        start = pl.multiple_of(full * block, block)
        visit(start, lambda shape: start + lax.broadcasted_iota(jnp.int32, shape, 1) < fill)

    done = first // block
    lax.fori_loop(0, done, plain(cache_rows), 0)
    offset = done * block - first
    visit(
        pl.multiple_of(cache_rows + done * block, block),
        lambda shape: offset + lax.broadcasted_iota(jnp.int32, shape, 1)
        <= lax.broadcasted_iota(jnp.int32, shape, 0),
    )
    for pair in range(heads // 2):
        both = [
            acc[2 * pair + u] / jnp.sum(total[2 * pair + u], axis=1, keepdims=True)
            for u in range(2)
        ]
        low = jnp.concatenate([head[:, :half] for head in both], axis=1)
        high = jnp.concatenate([head[:, half:] for head in both], axis=1)
        at = slice(pair * 2 * half, (pair + 1) * 2 * half)
        keep_ref[:, at] = jnp.where(core == 0, low, high).astype(keep_ref.dtype)
        send_ref[:, at] = jnp.where(core == 0, high, low).astype(send_ref.dtype)


def attend(info, query_blocks, key_blocks, value_blocks, block):
    planes, columns = len(key_blocks), len(value_blocks)
    chip_rows, features = query_blocks[0].shape
    rows, heads = columns * chip_rows, features // HEAD_SIZE
    total_rows = planes * columns * 2 * key_blocks[0].shape[2]
    out = jax.ShapeDtypeStruct((rows, features // 2), jnp.bfloat16)
    return pl.pallas_call(
        functools.partial(attention_kernel, planes, columns, block),
        out_shape=(out, out),
        in_specs=[pl.BlockSpec(memory_space=pltpu.SMEM)]
        + [pl.BlockSpec()] * (2 * columns + planes),
        out_specs=(pl.BlockSpec(), pl.BlockSpec()),
        scratch_shapes=[
            pltpu.VMEM((heads, rows, HEAD_SIZE), jnp.bfloat16),
            pltpu.VMEM((total_rows, HEAD_SIZE), jnp.bfloat16),
            pltpu.VMEM((total_rows, HEAD_SIZE), jnp.bfloat16),
            pltpu.VMEM((heads, rows, 1), jnp.float32),
            pltpu.VMEM((heads, rows, 128), jnp.float32),
            pltpu.VMEM((heads, rows, HEAD_SIZE), jnp.float32),
        ],
        compiler_params=pltpu.CompilerParams(vmem_limit_bytes=60 * 2**20),
    )(info, *query_blocks, *key_blocks, *value_blocks)


def expert_kernel(steps, own_ref, other_ref, gate_ref, up_ref, down_ref, *refs):
    keep_ref, send_ref, gated, lifted, activation = refs
    step = pl.program_id(0)
    count = own_ref.shape[0]

    @pl.when(step == 0)
    def _():
        gated[...] = jnp.zeros_like(gated)
        lifted[...] = jnp.zeros_like(lifted)

    @pl.when(step < steps)
    def _():
        both = jnp.concatenate([own_ref[...], other_ref[...]], axis=0)
        gated[...] += jnp.dot(both, gate_ref[...], preferred_element_type=jnp.float32)
        lifted[...] += jnp.dot(both, up_ref[...], preferred_element_type=jnp.float32)

    @pl.when(step == steps - 1)
    def _():
        activation[...] = (jax.nn.silu(gated[...]) * lifted[...]).astype(activation.dtype)

    @pl.when(step >= steps)
    def _():
        output = jnp.dot(activation[...], down_ref[...], preferred_element_type=jnp.float32)
        keep_ref[...] = output[:count].astype(keep_ref.dtype)
        send_ref[...] = output[count:].astype(send_ref.dtype)


def expert(own, other, gate, up, down):
    count, width = own.shape
    hidden_units = gate.shape[1]
    steps = 4
    part = width // steps
    row_spec = pl.BlockSpec((count, part), lambda i: (0, jnp.minimum(i, steps - 1)))
    weight_spec = pl.BlockSpec((part, hidden_units), lambda i: (jnp.minimum(i, steps - 1), 0))
    tail = lambda i: (0, jnp.maximum(i - steps, 0))
    out = jax.ShapeDtypeStruct((count, width), jnp.bfloat16)
    return pl.pallas_call(
        functools.partial(expert_kernel, steps),
        grid=(2 * steps,),
        out_shape=(out, out),
        in_specs=[row_spec, row_spec, weight_spec, weight_spec]
        + [pl.BlockSpec((hidden_units, part), tail)],
        out_specs=(pl.BlockSpec((count, part), tail), pl.BlockSpec((count, part), tail)),
        scratch_shapes=[
            pltpu.VMEM((2 * count, hidden_units), jnp.float32),
            pltpu.VMEM((2 * count, hidden_units), jnp.float32),
            pltpu.VMEM((2 * count, hidden_units), jnp.bfloat16),
        ],
        compiler_params=pltpu.CompilerParams(vmem_limit_bytes=20 * 2**20),
        cost_estimate=pl.CostEstimate(
            flops=12 * count * width * hidden_units,
            bytes_accessed=6 * width * hidden_units + 8 * count * width,
            transcendentals=2 * count * hidden_units,
        ),
    )(own, other, gate, up, down)


def x_spread(block):
    return [block] + [shifted(block, X, r) for r in range(1, CHIPS_X)]


def shards(
    hidden,
    queries,
    fresh_kv,
    cache_kv,
    cache_fill,
    out_proj,
    norm_gain,
    router_weight,
    expert_labels,
    gate_proj,
    up_proj,
    down_proj,
):
    planes = lax.axis_size("z")
    z, x = lax.axis_index("z"), lax.axis_index(X)
    core = lax.axis_index("core")
    tokens, width = hidden.shape[1:]
    heads_each = planes // 2
    middle = width // 2
    kv_heads = fresh_kv.shape[3] // HEAD_SIZE

    columns = [(x + r) % CHIPS_X for r in range(CHIPS_X)]
    joined = jnp.concatenate([cache_kv[0], fresh_kv[0]], axis=1)
    joined = jnp.moveaxis(
        joined.reshape(2, joined.shape[1], kv_heads, HEAD_SIZE), 2, 0
    )
    own_kv, own_queries = pick(joined, core), pick(queries[0].reshape(tokens, 2, -1), core, 1)
    other_kv = swapped(pick(joined, 1 - core), "core")
    other_queries = swapped(pick(queries[0].reshape(tokens, 2, -1), 1 - core, 1), "core")
    chip_kv = jnp.stack([own_kv, other_kv], axis=1)
    chip_queries = jnp.concatenate([own_queries, other_queries], axis=0).reshape(
        2 * tokens, heads_each, CHIPS_X, HEAD_SIZE
    )
    key_column = jnp.stack(x_spread(chip_kv[0]))
    query_blocks = [pick(chip_queries, x, 2).reshape(2 * tokens, -1)] + [
        shifted(pick(chip_queries, columns[r], 2).reshape(2 * tokens, -1), X, r)
        for r in range(1, CHIPS_X)
    ]
    value_planes = [chip_kv[1]] + [shifted(chip_kv[1], "z", k) for k in range(1, planes)]
    key_blocks = [key_column] * planes
    for k in range(1, planes // 2 + 1):
        key_blocks[k] = shifted(key_blocks[k - 1], "z", 1)
        if k < planes - k:
            key_blocks[planes - k] = shifted(key_blocks[(planes - k + 1) % planes], "z", -1)
        if k == 1:
            key_blocks, value_planes, own_rows = lax.optimization_barrier(
                (key_blocks, value_planes, out_proj[0])
            )
            value_blocks = x_spread(jnp.stack(value_planes))
        if k == 3:
            key_blocks, query_blocks, value_blocks[1] = lax.optimization_barrier(
                (key_blocks, query_blocks, value_blocks[1])
            )
    weight_rows = lax.all_gather(own_rows, "z", axis=0, tiled=True)
    info = jnp.stack([z, x, core, cache_fill[0]]).astype(jnp.int32)
    block = min(1024, planes * 8 * (joined.shape[2] - tokens))
    keep, send = attend(info, query_blocks, key_blocks, value_blocks, block)
    features = in_order(core, keep, swapped(send, "core"), 1)
    features = features.reshape(CHIPS_X, 2 * tokens, features.shape[1])

    def projection(step):
        both = jnp.dot(
            pick(features, (x + step) % CHIPS_X), weight_rows, preferred_element_type=jnp.float32
        ).reshape(2, tokens, width)
        return pick(both, core) + swapped(
            pick(both, 1 - core).astype(jnp.bfloat16), "core"
        ).astype(jnp.float32)

    def sent(part, by):
        return shifted(part.astype(jnp.bfloat16), X, by).astype(jnp.float32)

    opposite = projection(2)
    relay_up, relay_down = sent(opposite[:, :middle], 1), sent(opposite[:, middle:], -1)
    above, below = projection(1), projection(3)
    low = sent(below[:, :middle], -1) + sent(above[:, :middle] + relay_up, 1)
    high = sent(above[:, middle:], 1) + sent(below[:, middle:] + relay_down, -1)
    mixed = (
        hidden[0].astype(jnp.float32) + projection(0) + jnp.concatenate([low, high], axis=1)
    )
    inverse = lax.rsqrt(jnp.mean(mixed * mixed, axis=1, keepdims=True) + 1e-06)
    normed = (mixed * inverse * norm_gain[0].astype(jnp.float32)[None, :]).astype(jnp.bfloat16)

    label_rows = expert_labels[0]
    experts = planes * 2
    airborne = label_rows < experts
    chosen = jnp.sum(jnp.where(airborne, label_rows, 0), axis=1)
    capacity = 8
    member = (chosen[:, None] == jnp.arange(experts, dtype=jnp.int32)[None, :]).astype(jnp.int32)
    earlier = jnp.cumsum(member, axis=0) - member
    code = chosen * capacity + jnp.sum(earlier * member, axis=1)
    table = (
        code[None, :] == jnp.arange(experts * capacity, dtype=jnp.int32)[:, None]
    ).astype(jnp.bfloat16)
    packed = jnp.dot(table, normed, preferred_element_type=jnp.float32).astype(jnp.bfloat16)

    logits = jnp.dot(normed, router_weight[0], preferred_element_type=jnp.float32)
    matches = label_rows[:, :, None] == jnp.arange(EXPERTS, dtype=jnp.int32)[None, None, :]
    picked = jnp.sum(jnp.where(matches, logits[:, None, :], 0.0), axis=2)
    probabilities = jax.nn.softmax(picked, axis=1)
    combine = jnp.sum(jnp.where(airborne, probabilities, 0.0), axis=1)

    weights = (gate_proj[0, 0], up_proj[0, 0], down_proj[0, 0])
    near = lax.all_to_all(packed, GROUP, split_axis=0, concat_axis=0, tiled=True)
    near_other = swapped(near, "core")
    far = swapped(near, "xl")
    near_keep, near_send = expert(near, near_other, *weights)
    far, near_keep, near_send = lax.optimization_barrier((far, near_keep, near_send))
    far_keep, far_send = expert(far, swapped(far, "core"), *weights)

    def wide(array):
        return array.astype(jnp.float32)

    far_sum = (wide(far_keep) + wide(swapped(far_send, "core"))).astype(jnp.bfloat16)
    near_sum = wide(near_keep) + wide(swapped(near_send, "core"))
    summed = (near_sum + wide(swapped(far_sum, "xl"))).astype(jnp.bfloat16)
    returned = lax.all_to_all(summed, GROUP, split_axis=0, concat_axis=0, tiled=True)
    routed = lax.dot_general(
        table, returned, (((0,), (0,)), ((), ())), preferred_element_type=jnp.float32
    )
    result = (mixed + combine[:, None] * routed).astype(jnp.bfloat16)
    return shifted(result[None], "section", 1)


def solution(mesh):
    sections, devices = mesh.devices.shape
    planes = devices // (2 * CHIPS_X)
    fine = Mesh(
        mesh.devices.reshape(sections, planes, 2, 2, 2), ("section",) + EXPERT
    )
    in_specs = (
        P("section", EXPERT, None),
        P("section", EXPERT, None),
        P("section", None, EXPERT, None),
        P("section", None, EXPERT, None),
        P("section"),
        P("section", EXPERT, None),
        P("section", None),
        P("section", None, None),
        P("section", EXPERT, None),
        P("section", EXPERT, None, None),
        P("section", EXPERT, None, None),
        P("section", EXPERT, None, None),
    )
    out_specs = P("section", EXPERT, None)
    return jax.shard_map(shards, mesh=fine, in_specs=in_specs, out_specs=out_specs, check_vma=False)
```

```python
import functools
import math

import jax
import jax.numpy as jnp
from jax import lax
from jax.experimental import pallas as pl
from jax.experimental.pallas import tpu as pltpu
from jax.sharding import Mesh
from jax.sharding import PartitionSpec as P

EXPERTS = 128
HEAD_SIZE = 128
SPLIT = 4
CHIPS_X = 4
X = ("xh", "xl")
EXPERT = ("z", "xh", "xl", "core")
GROUP = ("z", "xh")


def shifted(shard, axis, by):
    length = lax.axis_size(axis)
    return lax.ppermute(shard, axis, [(i, (i + by) % length) for i in range(length)])


def swapped(shard, axis):
    return lax.ppermute(shard, axis, [(0, 1), (1, 0)])


def in_order(index, own, other, axis):
    return jnp.where(
        index == 0,
        jnp.concatenate([own, other], axis=axis),
        jnp.concatenate([other, own], axis=axis),
    )


def pick(array, index, axis=0):
    return lax.dynamic_index_in_dim(array, index, axis, keepdims=False)


def attention_kernel(planes, columns, block, info_ref, *refs):
    query_blocks = refs[:columns]
    key_blocks = refs[columns : columns + planes]
    value_blocks = refs[columns + planes : 2 * columns + planes]
    keep_ref, send_ref, query_ref, keys, values, top, total, acc = refs[2 * columns + planes :]
    z, x, core, fill = info_ref[0], info_ref[1], info_ref[2], info_ref[3]
    local = key_blocks[0].shape[2]
    fresh = (2 * local) // 3
    cached = local - fresh
    cache_rows = 2 * planes * columns * cached
    heads = query_ref.shape[0]
    half = HEAD_SIZE // 2
    first = z * (2 * columns * fresh)
    for r in range(columns):
        from_x = lax.rem(x - r + columns, columns)
        for n in range(2):
            from_core = core if n == 0 else 1 - core
            at = pl.multiple_of((from_x * 2 + from_core) * fresh, fresh)
            for head in range(heads):
                query_ref[head, pl.ds(at, fresh), :] = query_blocks[r][
                    n * fresh : (n + 1) * fresh, head * HEAD_SIZE : (head + 1) * HEAD_SIZE
                ]
    for k in range(planes):
        plane = lax.rem(z - k + planes, planes)
        for r in range(columns):
            chip = plane * columns + lax.rem(x - r + columns, columns)
            for n in range(2):
                device = chip * 2 + (core if n == 0 else 1 - core)
                at_cache = pl.multiple_of(device * cached, cached)
                at_fresh = pl.multiple_of(cache_rows + device * fresh, fresh)
                for held, part in ((keys, key_blocks[k]), (values, value_blocks[r])):
                    where = (r, n) if held is keys else (k, n)
                    held[pl.ds(at_cache, cached), :] = part[where[0], where[1], :cached, :]
                    held[pl.ds(at_fresh, fresh), :] = part[where[0], where[1], cached:, :]
    rate = math.log2(math.e) / math.sqrt(HEAD_SIZE)

    def score(head, start):
        return lax.dot_general(
            query_ref[head],
            keys[pl.ds(start, block), :],
            (((1,), (1,)), ((), ())),
            preferred_element_type=jnp.float32,
        )

    def visit(start, visible):
        ahead = score(0, start)
        for head in range(heads):
            scores = ahead
            if head + 1 < heads:
                ahead = score(head + 1, start)
            if visible is not None:
                mask = visible(scores.shape)
                scores = jnp.where(mask, scores, -1e30)
            before = top[head]
            high = jnp.maximum(before, jnp.max(scores, axis=1, keepdims=True))
            weights = jnp.exp2((scores - high) * rate)
            if visible is not None:
                weights = jnp.where(mask, weights, 0.0)
            factor = jnp.exp2((before - high) * rate)
            part = weights[:, :128]
            for n in range(1, block // 128):
                part = part + weights[:, n * 128 : (n + 1) * 128]
            total[head] = total[head] * factor + part
            top[head] = high
            acc[head] = acc[head] * factor + jnp.dot(
                weights.astype(jnp.bfloat16),
                values[pl.ds(start, block), :],
                preferred_element_type=jnp.float32,
            )

    top[...] = jnp.full_like(top, -1e30)
    total[...] = jnp.zeros_like(total)
    acc[...] = jnp.zeros_like(acc)

    def plain(base):
        def body(n, unused):
            visit(pl.multiple_of(base + n * block, block), None)
            return unused

        return body

    full = fill // block
    lax.fori_loop(0, full, plain(0), 0)

    @pl.when(fill > full * block)
    def _():
        start = pl.multiple_of(full * block, block)
        visit(start, lambda shape: start + lax.broadcasted_iota(jnp.int32, shape, 1) < fill)

    done = first // block
    lax.fori_loop(0, done, plain(cache_rows), 0)
    offset = done * block - first
    visit(
        pl.multiple_of(cache_rows + done * block, block),
        lambda shape: offset + lax.broadcasted_iota(jnp.int32, shape, 1)
        <= lax.broadcasted_iota(jnp.int32, shape, 0),
    )
    for pair in range(heads // 2):
        both = [
            acc[2 * pair + u] / jnp.sum(total[2 * pair + u], axis=1, keepdims=True)
            for u in range(2)
        ]
        low = jnp.concatenate([head[:, :half] for head in both], axis=1)
        high = jnp.concatenate([head[:, half:] for head in both], axis=1)
        at = slice(pair * 2 * half, (pair + 1) * 2 * half)
        keep_ref[:, at] = jnp.where(core == 0, low, high).astype(keep_ref.dtype)
        send_ref[:, at] = jnp.where(core == 0, high, low).astype(send_ref.dtype)


def attend(info, query_blocks, key_blocks, value_blocks, block):
    planes, columns = len(key_blocks), len(value_blocks)
    chip_rows, features = query_blocks[0].shape
    rows, heads = columns * chip_rows, features // HEAD_SIZE
    total_rows = planes * columns * 2 * key_blocks[0].shape[2]
    out = jax.ShapeDtypeStruct((rows, features // 2), jnp.bfloat16)
    return pl.pallas_call(
        functools.partial(attention_kernel, planes, columns, block),
        out_shape=(out, out),
        in_specs=[pl.BlockSpec(memory_space=pltpu.SMEM)]
        + [pl.BlockSpec()] * (2 * columns + planes),
        out_specs=(pl.BlockSpec(), pl.BlockSpec()),
        scratch_shapes=[
            pltpu.VMEM((heads, rows, HEAD_SIZE), jnp.bfloat16),
            pltpu.VMEM((total_rows, HEAD_SIZE), jnp.bfloat16),
            pltpu.VMEM((total_rows, HEAD_SIZE), jnp.bfloat16),
            pltpu.VMEM((heads, rows, 1), jnp.float32),
            pltpu.VMEM((heads, rows, 128), jnp.float32),
            pltpu.VMEM((heads, rows, HEAD_SIZE), jnp.float32),
        ],
        compiler_params=pltpu.CompilerParams(vmem_limit_bytes=60 * 2**20),
    )(info, *query_blocks, *key_blocks, *value_blocks)


def expert_kernel(steps, own_ref, other_ref, gate_ref, up_ref, down_ref, *refs):
    keep_ref, send_ref, gated, lifted, activation = refs
    step = pl.program_id(0)
    count = own_ref.shape[0]

    @pl.when(step == 0)
    def _():
        gated[...] = jnp.zeros_like(gated)
        lifted[...] = jnp.zeros_like(lifted)

    @pl.when(step < steps)
    def _():
        both = jnp.concatenate([own_ref[...], other_ref[...]], axis=0)
        gated[...] += jnp.dot(both, gate_ref[...], preferred_element_type=jnp.float32)
        lifted[...] += jnp.dot(both, up_ref[...], preferred_element_type=jnp.float32)

    @pl.when(step == steps - 1)
    def _():
        activation[...] = (jax.nn.silu(gated[...]) * lifted[...]).astype(activation.dtype)

    @pl.when(step >= steps)
    def _():
        output = jnp.dot(activation[...], down_ref[...], preferred_element_type=jnp.float32)
        keep_ref[...] = output[:count].astype(keep_ref.dtype)
        send_ref[...] = output[count:].astype(send_ref.dtype)


def expert(own, other, gate, up, down):
    count, width = own.shape
    hidden_units = gate.shape[1]
    steps = 4
    part = width // steps
    row_spec = pl.BlockSpec((count, part), lambda i: (0, jnp.minimum(i, steps - 1)))
    weight_spec = pl.BlockSpec((part, hidden_units), lambda i: (jnp.minimum(i, steps - 1), 0))
    tail = lambda i: (0, jnp.maximum(i - steps, 0))
    out = jax.ShapeDtypeStruct((count, width), jnp.bfloat16)
    return pl.pallas_call(
        functools.partial(expert_kernel, steps),
        grid=(2 * steps,),
        out_shape=(out, out),
        in_specs=[row_spec, row_spec, weight_spec, weight_spec]
        + [pl.BlockSpec((hidden_units, part), tail)],
        out_specs=(pl.BlockSpec((count, part), tail), pl.BlockSpec((count, part), tail)),
        scratch_shapes=[
            pltpu.VMEM((2 * count, hidden_units), jnp.float32),
            pltpu.VMEM((2 * count, hidden_units), jnp.float32),
            pltpu.VMEM((2 * count, hidden_units), jnp.bfloat16),
        ],
        compiler_params=pltpu.CompilerParams(vmem_limit_bytes=20 * 2**20),
        cost_estimate=pl.CostEstimate(
            flops=12 * count * width * hidden_units,
            bytes_accessed=6 * width * hidden_units + 8 * count * width,
            transcendentals=2 * count * hidden_units,
        ),
    )(own, other, gate, up, down)


def x_spread(block):
    return [block] + [shifted(block, X, r) for r in range(1, CHIPS_X)]


def shards(
    hidden,
    queries,
    fresh_kv,
    cache_kv,
    cache_fill,
    out_proj,
    norm_gain,
    router_weight,
    expert_labels,
    gate_proj,
    up_proj,
    down_proj,
):
    planes = lax.axis_size("z")
    z, x = lax.axis_index("z"), lax.axis_index(X)
    core = lax.axis_index("core")
    tokens, width = hidden.shape[1:]
    heads_each = planes // 2
    middle = width // 2
    kv_heads = fresh_kv.shape[3] // HEAD_SIZE

    columns = [(x + r) % CHIPS_X for r in range(CHIPS_X)]
    joined = jnp.concatenate([cache_kv[0], fresh_kv[0]], axis=1)
    joined = jnp.moveaxis(
        joined.reshape(2, joined.shape[1], kv_heads, HEAD_SIZE), 2, 0
    )
    own_kv, own_queries = pick(joined, core), pick(queries[0].reshape(tokens, 2, -1), core, 1)
    other_kv = swapped(pick(joined, 1 - core), "core")
    other_queries = swapped(pick(queries[0].reshape(tokens, 2, -1), 1 - core, 1), "core")
    chip_kv = jnp.stack([own_kv, other_kv], axis=1)
    chip_queries = jnp.concatenate([own_queries, other_queries], axis=0).reshape(
        2 * tokens, heads_each, CHIPS_X, HEAD_SIZE
    )
    key_column = jnp.stack(x_spread(chip_kv[0]))
    query_blocks = [pick(chip_queries, x, 2).reshape(2 * tokens, -1)] + [
        shifted(pick(chip_queries, columns[r], 2).reshape(2 * tokens, -1), X, r)
        for r in range(1, CHIPS_X)
    ]
    value_planes = [chip_kv[1]] + [shifted(chip_kv[1], "z", k) for k in range(1, planes)]
    key_column, value_planes, query_blocks, own_rows = lax.optimization_barrier(
        (key_column, value_planes, query_blocks, out_proj[0])
    )
    value_blocks = x_spread(jnp.stack(value_planes))
    key_blocks = [key_column] * planes
    for k in range(1, planes // 2 + 1):
        key_blocks[k] = shifted(key_blocks[k - 1], "z", 1)
        if k < planes - k:
            key_blocks[planes - k] = shifted(key_blocks[(planes - k + 1) % planes], "z", -1)
        if k == 3:
            key_blocks, value_blocks[1], value_blocks[3] = lax.optimization_barrier(
                (key_blocks, value_blocks[1], value_blocks[3])
            )
    weight_rows = lax.all_gather(own_rows, "z", axis=0, tiled=True)
    info = jnp.stack([z, x, core, cache_fill[0]]).astype(jnp.int32)
    block = min(1024, planes * 8 * (joined.shape[2] - tokens))
    keep, send = attend(info, query_blocks, key_blocks, value_blocks, block)
    features = in_order(core, keep, swapped(send, "core"), 1)
    features = features.reshape(CHIPS_X, 2 * tokens, features.shape[1])

    def projection(step):
        both = jnp.dot(
            pick(features, (x + step) % CHIPS_X), weight_rows, preferred_element_type=jnp.float32
        ).reshape(2, tokens, width)
        return pick(both, core) + swapped(
            pick(both, 1 - core).astype(jnp.bfloat16), "core"
        ).astype(jnp.float32)

    def sent(part, by):
        return shifted(part.astype(jnp.bfloat16), X, by).astype(jnp.float32)

    opposite = projection(2)
    relay_up, relay_down = sent(opposite[:, :middle], 1), sent(opposite[:, middle:], -1)
    above, below = projection(1), projection(3)
    low = sent(below[:, :middle], -1) + sent(above[:, :middle] + relay_up, 1)
    high = sent(above[:, middle:], 1) + sent(below[:, middle:] + relay_down, -1)
    mixed = (
        hidden[0].astype(jnp.float32) + projection(0) + jnp.concatenate([low, high], axis=1)
    )
    inverse = lax.rsqrt(jnp.mean(mixed * mixed, axis=1, keepdims=True) + 1e-06)
    normed = (mixed * inverse * norm_gain[0].astype(jnp.float32)[None, :]).astype(jnp.bfloat16)

    label_rows = expert_labels[0]
    experts = planes * 2
    airborne = label_rows < experts
    chosen = jnp.sum(jnp.where(airborne, label_rows, 0), axis=1)
    capacity = 8
    member = (chosen[:, None] == jnp.arange(experts, dtype=jnp.int32)[None, :]).astype(jnp.int32)
    earlier = jnp.cumsum(member, axis=0) - member
    code = chosen * capacity + jnp.sum(earlier * member, axis=1)
    table = (
        code[None, :] == jnp.arange(experts * capacity, dtype=jnp.int32)[:, None]
    ).astype(jnp.bfloat16)
    packed = jnp.dot(table, normed, preferred_element_type=jnp.float32).astype(jnp.bfloat16)

    logits = jnp.dot(normed, router_weight[0], preferred_element_type=jnp.float32)
    matches = label_rows[:, :, None] == jnp.arange(EXPERTS, dtype=jnp.int32)[None, None, :]
    picked = jnp.sum(jnp.where(matches, logits[:, None, :], 0.0), axis=2)
    probabilities = jax.nn.softmax(picked, axis=1)
    combine = jnp.sum(jnp.where(airborne, probabilities, 0.0), axis=1)

    weights = (gate_proj[0, 0], up_proj[0, 0], down_proj[0, 0])
    near = lax.all_to_all(packed, GROUP, split_axis=0, concat_axis=0, tiled=True)
    near_other = swapped(near, "core")
    far = swapped(near, "xl")
    near_keep, near_send = expert(near, near_other, *weights)
    far, near_keep, near_send = lax.optimization_barrier((far, near_keep, near_send))
    far_keep, far_send = expert(far, swapped(far, "core"), *weights)

    def wide(array):
        return array.astype(jnp.float32)

    far_sum = (wide(far_keep) + wide(swapped(far_send, "core"))).astype(jnp.bfloat16)
    near_sum = wide(near_keep) + wide(swapped(near_send, "core"))
    summed = (near_sum + wide(swapped(far_sum, "xl"))).astype(jnp.bfloat16)
    returned = lax.all_to_all(summed, GROUP, split_axis=0, concat_axis=0, tiled=True)
    routed = lax.dot_general(
        table, returned, (((0,), (0,)), ((), ())), preferred_element_type=jnp.float32
    )
    result = (mixed + combine[:, None] * routed).astype(jnp.bfloat16)
    return shifted(result[None], "section", 1)


def solution(mesh):
    sections, devices = mesh.devices.shape
    planes = devices // (2 * CHIPS_X)
    fine = Mesh(
        mesh.devices.reshape(sections, planes, 2, 2, 2), ("section",) + EXPERT
    )
    in_specs = (
        P("section", EXPERT, None),
        P("section", EXPERT, None),
        P("section", None, EXPERT, None),
        P("section", None, EXPERT, None),
        P("section"),
        P("section", EXPERT, None),
        P("section", None),
        P("section", None, None),
        P("section", EXPERT, None),
        P("section", EXPERT, None, None),
        P("section", EXPERT, None, None),
        P("section", EXPERT, None, None),
    )
    out_specs = P("section", EXPERT, None)
    return jax.shard_map(shards, mesh=fine, in_specs=in_specs, out_specs=out_specs, check_vma=False)
```
